32 devices in a mesh: lyr: 2 (over core), strip: 16 (over z, y, x).
Axes of the slice: x: 2, y: 2, z: 4, core: 2. Of those that a mesh axis runs over, the one named last changes fastest.
Arguments:
- nodes: bfloat16 [2, 2, 64, 128, 128], P('lyr', None, None, 'strip'), may hold values from -6 to 6
- upstream: bfloat16 [2, 2, 64, 128, 128], P('lyr', None, None, 'strip'), may hold values from -6 to 6
- usage: int32 [2, 2, 128, 128], P('lyr', None, 'strip'), may hold values from 0 to 15
- blockage: int32 [2, 2, 2, 128, 128], P('lyr', None, None, 'strip'), may hold values 0 or 1
- capacity: int32 [2, 2, 2, 128, 128], P('lyr', None, None, 'strip'), may hold values from 1 to 8
- w_src: bfloat16 [2, 128, 64], replicated, may hold values from -0.75 to 0.75
- w_dst: bfloat16 [2, 128, 64], replicated, may hold values from -0.75 to 0.75
- w_out: bfloat16 [2, 64, 128], replicated, may hold values from -0.5 to 0.5
Outputs:
- grad_nodes: bfloat16 [2, 2, 64, 128, 128], P('lyr', None, None, 'strip')
- grad_src: float32 [2, 128, 64], replicated
- grad_dst: float32 [2, 128, 64], replicated
- grad_out: float32 [2, 64, 128], replicated
The draws below stay inside these ranges and needn't reach their ends.
All inputs are finite; a program needn't handle non-finite values. No bound on the sum of `blockage` on one device may be relied on, other than what follows from the above.
Results may differ from the reference program's by a relative error of at most 0.0058.
Values may be sent and summed in bfloat16 or wider, within the bound.
A program may use at most 128 MiB of HBM per device.

```python
import jax
import jax.numpy as jnp
from jax import lax

F = 64
H = 128
G = 128
PAIRS = 2


def plant(entries, own_key, smallest, largest):
    spot = [jax.random.randint(jax.random.fold_in(own_key, axis), (), 0, length) for axis, length in enumerate(entries.shape)]
    longest = entries.shape.index(max(entries.shape))
    neighbour = spot[:longest] + [(spot[longest] + 1) % entries.shape[longest]] + spot[longest + 1:]
    return entries.at[tuple(spot)].set(smallest).at[tuple(neighbour)].set(largest)


def block_scale(key, extent, shards, low, high):
    factor_of = 1.0
    for dim, blocks in shards:
        draws = jax.random.uniform(jax.random.fold_in(jax.random.fold_in(key, 6), dim), (blocks,), jnp.float32, low / len(shards), high / len(shards))
        factor_of = factor_of * jnp.repeat(jnp.exp(draws), extent[dim] // blocks).reshape((-1,) + (1,) * (len(extent) - 1 - dim))
    return factor_of


def gaussian(key, extent, scale, bound, split=(), dtype=jnp.bfloat16):
    loudness = block_scale(key, extent, split, -0.22, 0.18) if split else 1.0
    values = jax.random.normal(key, extent, jnp.float32) * scale * loudness
    return jnp.minimum(jnp.maximum(values, -bound), bound).astype(dtype)


def setup_inputs(seed: int = 0) -> dict:
    keys = jax.random.split(jax.random.key(seed), 9)
    return {
        "nodes": gaussian(keys[0], (PAIRS, 2, F, G, G), 1.0, 6.0, ((0, 2), (3, 16))),
        "upstream": gaussian(keys[1], (PAIRS, 2, F, G, G), 1.0, 6.0, ((0, 2), (3, 16))),
        "usage": plant(jax.random.randint(keys[2], (PAIRS, 2, G, G), 0, 16), jax.random.fold_in(keys[2], 1), 0, 15).astype(jnp.int32),
        "blockage": plant((jax.random.randint(keys[3], (PAIRS, 2, 2, G, G), 0, 8) < 1).astype(jnp.int32), jax.random.fold_in(keys[3], 1), 0, 1),
        "capacity": plant(jax.random.randint(keys[4], (PAIRS, 2, 2, G, G), 1, 9), jax.random.fold_in(keys[4], 1), 1, 8).astype(jnp.int32),
        "w_src": gaussian(keys[5], (2, H, F), F ** -0.5, 0.75),
        "w_dst": gaussian(keys[6], (2, H, F), F ** -0.5, 0.75),
        "w_out": gaussian(keys[7], (2, F, H), H ** -0.5, 0.5),
    }


def edge_grads(w_src, w_dst, w_out, x_u, x_v, d_u, d_v, gate):
    feat, rows, cols = x_u.shape
    count = rows * cols
    flat_u = x_u.reshape(feat, count)
    flat_v = x_v.reshape(feat, count)
    pre = jnp.dot(w_src, flat_u, preferred_element_type=jnp.float32) + jnp.dot(w_dst, flat_v, preferred_element_type=jnp.float32)
    sigma = jax.nn.sigmoid(pre)
    act = (pre * sigma).astype(jnp.bfloat16)
    slope = sigma * (1.0 + pre * (1.0 - sigma))
    diff = d_v.astype(jnp.float32) - d_u.astype(jnp.float32)
    g_msg = (gate[None] * diff).reshape(feat, count).astype(jnp.bfloat16)
    g_act = lax.dot_general(w_out, g_msg, (((0,), (0,)), ((), ())), preferred_element_type=jnp.float32)
    g_pre = (g_act * slope).astype(jnp.bfloat16)
    g_out = lax.dot_general(g_msg, act, (((1,), (1,)), ((), ())), preferred_element_type=jnp.float32)
    g_src = lax.dot_general(g_pre, flat_u, (((1,), (1,)), ((), ())), preferred_element_type=jnp.float32)
    g_dst = lax.dot_general(g_pre, flat_v, (((1,), (1,)), ((), ())), preferred_element_type=jnp.float32)
    gx_u = lax.dot_general(w_src, g_pre, (((0,), (0,)), ((), ())), preferred_element_type=jnp.float32)
    gx_v = lax.dot_general(w_dst, g_pre, (((0,), (0,)), ((), ())), preferred_element_type=jnp.float32)
    return (gx_u.reshape(feat, rows, cols), gx_v.reshape(feat, rows, cols), (g_src, g_dst, g_out))

def reference(nodes, upstream, usage, blockage, capacity, w_src, w_dst, w_out):
    damp = lax.rsqrt(1.0 + usage.astype(jnp.float32))[:, :, None]
    feats = (nodes.astype(jnp.float32) * damp).astype(jnp.bfloat16)
    gates = (1 - blockage).astype(jnp.float32) * capacity.astype(jnp.float32) * 0.25
    pairs = nodes.shape[0]
    feat = nodes.shape[2]
    side = nodes.shape[4]
    inside = (jnp.arange(side) < side - 1).astype(jnp.float32)
    accum = [[jnp.zeros((feat, side, side), jnp.float32) for j in range(2)] for p in range(pairs)]
    totals = [None, None]

    def add_weights(kind, parts):
        if totals[kind] is None:
            totals[kind] = parts
        else:
            totals[kind] = tuple((a + b for a, b in zip(totals[kind], parts)))
    for p in range(pairs):
        for j in range(2):
            x_u = feats[p, j]
            d_u = upstream[p, j]
            if (j + p) % 2 == 0:
                x_v = jnp.concatenate((x_u[:, 1:, :], jnp.zeros((feat, 1, side), jnp.bfloat16)), 1)
                d_v = jnp.concatenate((d_u[:, 1:, :], jnp.zeros((feat, 1, side), jnp.bfloat16)), 1)
                gate = gates[p, j, 0] * inside[:, None]
                gu, gv, parts = edge_grads(w_src[0], w_dst[0], w_out[0], x_u, x_v, d_u, d_v, gate)
                accum[p][j] = accum[p][j] + gu + jnp.concatenate((jnp.zeros((feat, 1, side), jnp.float32), gv[:, :-1, :]), 1)
            else:
                x_v = jnp.concatenate((x_u[:, :, 1:], jnp.zeros((feat, side, 1), jnp.bfloat16)), 2)
                d_v = jnp.concatenate((d_u[:, :, 1:], jnp.zeros((feat, side, 1), jnp.bfloat16)), 2)
                gate = gates[p, j, 0] * inside[None, :]
                gu, gv, parts = edge_grads(w_src[0], w_dst[0], w_out[0], x_u, x_v, d_u, d_v, gate)
                accum[p][j] = accum[p][j] + gu + jnp.concatenate((jnp.zeros((feat, side, 1), jnp.float32), gv[:, :, :-1]), 2)
            add_weights(0, parts)
            if j == 0:
                gu, gv, parts = edge_grads(w_src[1], w_dst[1], w_out[1], x_u, feats[p, 1], d_u, upstream[p, 1], gates[p, 0, 1])
                accum[p][0] = accum[p][0] + gu
                accum[p][1] = accum[p][1] + gv
                add_weights(1, parts)
            elif p < pairs - 1:
                x_v = jnp.swapaxes(feats[p + 1, 0], 1, 2)
                d_v = jnp.swapaxes(upstream[p + 1, 0], 1, 2)
                gu, gv, parts = edge_grads(w_src[1], w_dst[1], w_out[1], x_u, x_v, d_u, d_v, gates[p, 1, 1])
                accum[p][1] = accum[p][1] + gu
                accum[p + 1][0] = accum[p + 1][0] + jnp.swapaxes(gv, 1, 2)
                add_weights(1, parts)
    node_sum = jnp.stack([jnp.stack(accum[p]) for p in range(pairs)])
    grad_nodes = (upstream.astype(jnp.float32) + damp * node_sum).astype(jnp.bfloat16)
    scale = 1.0 / jnp.sqrt(jnp.float32(2 * pairs * side * side))
    grad_src = jnp.stack((totals[0][0], totals[1][0])) * scale
    grad_dst = jnp.stack((totals[0][1], totals[1][1])) * scale
    grad_out = jnp.stack((totals[0][2], totals[1][2])) * scale
    return (grad_nodes, grad_src, grad_dst, grad_out)
```

```python
import functools
import math

import jax
import jax.numpy as jnp
from jax import lax
from jax.experimental import pallas as pl
from jax.experimental.pallas import tpu as pltpu
from jax.sharding import PartitionSpec as P

MESH = pl.DeviceIdType.MESH
F32 = jnp.float32
BF16 = jnp.bfloat16
TILE = 16


def mm(a, b):
    return jnp.dot(a, b, preferred_element_type=F32)


def edges(xu, xv, gate, w):
    both = jnp.concatenate((xu, xv), 1)
    y = mm(both, w)
    half = w.shape[1] // 2
    pre, raw = y[:, :half], y[:, half:]
    s = 0.5 * jnp.tanh(0.5 * pre) + 0.5
    act = pre * s
    slope = s + act * (1.0 - s)
    gate = gate.astype(F32)
    return both, (gate * raw * slope).astype(BF16), (gate * act).astype(BF16)


def weight_sums(gp, ga, both):
    left = jnp.concatenate((gp, ga), 1)
    return lax.dot_general(left, both, (((0,), (0,)), ((), ())), preferred_element_type=F32)


def kernel(
    pairs, strips, rows, cols, chunk,
    xd, s_up, s_dn, gb, w1, pw, vw,
    acc, w_sum,
    prev_x, next_x, prev_g, below, above, gps, wacc, wpart, wrecv, wres,
    halo_send, halo_recv, cross_send, cross_recv, red_send, red_recv,
):
    p = lax.axis_index("lyr")
    s = lax.axis_index("strip")
    devices = pairs * strips
    flat = p * strips + s
    owners = wpart.shape[0]
    cells = rows * cols
    step = chunk * cols
    square = rows * rows

    def place(k):
        target = lax.rem(flat + k, devices)
        return target, (lax.div(target, strips), lax.rem(target, strips))

    barrier = pltpu.get_barrier_semaphore()

    @pl.loop(1, devices)
    def _(k):
        pl.semaphore_signal(barrier, inc=1, device_id=place(k)[1], device_id_type=MESH)

    pl.semaphore_wait(barrier, devices - 1)

    jr = lax.rem(p, 2)
    jc = 1 - jr

    def send(src, dst, a, b, to):
        copy = pltpu.make_async_remote_copy(
            src_ref=src, dst_ref=dst, send_sem=a, recv_sem=b, device_id=to, device_id_type=MESH
        )
        copy.start()
        return copy

    def wait_bytes(ref, sem):
        pltpu.make_async_copy(ref, ref, sem).wait()

    @pl.loop(0, strips)
    def _(k):
        t = lax.rem(s + k, strips)

        @pl.when(p < pairs - 1)
        def _():
            send(s_up.at[t], below.at[s], cross_send.at[0], cross_recv.at[0], (p + 1, t))

        @pl.when(p > 0)
        def _():
            send(s_dn.at[t], above.at[s], cross_send.at[1], cross_recv.at[1], (p - 1, t))

    after = (p, lax.rem(s + 1, strips))
    before = (p, lax.rem(s + strips - 1, strips))
    last = pl.ds(cells - cols, cols)
    halos = (
        send(xd.at[jr, pl.ds(0, cols)], next_x, halo_send.at[0], halo_recv.at[0], before),
        send(xd.at[jr, last], prev_x, halo_send.at[1], halo_recv.at[1], after),
        send(gb.at[jr, last], prev_g, halo_send.at[2], halo_recv.at[2], after),
    )

    starts = range(0, cells, step)
    for at in starts:
        here = pl.ds(at, step)
        both, gp, ga = edges(xd[0, here], xd[1, here], gb[2, here], w1[1])
        acc[here] = mm(gp, vw[0])
        sums = weight_sums(gp, ga, both)
        wacc[1] = sums if at == 0 else wacc[1] + sums
    for at in starts:
        here = pl.ds(at, step)
        xu = xd[jc, here]
        wide = xu.astype(F32)
        xv = jnp.concatenate((wide[1:], wide[:1]), 0).astype(BF16)
        both, gp, ga = edges(xu, xv, gb[jc, here], w1[0])
        wide = gp.astype(F32)
        turned = jnp.concatenate((wide[-1:], wide[:-1]), 0).astype(BF16)
        acc[here] += mm(jnp.concatenate((gp, turned), 1), pw[jc])
        sums = weight_sums(gp, ga, both)
        wacc[0] = sums if at == 0 else wacc[0] + sums
    for copy in halos:
        copy.wait()
    _, gp, _ = edges(prev_x[...], xd[jr, pl.ds(0, cols)], prev_g[...], w1[0])
    gps[pl.ds(0, cols)] = gp
    for at in starts:
        here = pl.ds(at, step)
        if at + step < cells:
            xv = xd[jr, pl.ds(at + cols, step)]
        elif step > cols:
            xv = jnp.concatenate((xd[jr, pl.ds(at + cols, step - cols)], next_x[...]), 0)
        else:
            xv = next_x[...]
        both, gp, ga = edges(xd[jr, here], xv, gb[jr, here], w1[0])
        gps[pl.ds(at + cols, step)] = gp
        acc[here] += mm(jnp.concatenate((gp, gps[here]), 1), pw[jr])
        wacc[0] += weight_sums(gp, ga, both)

    def arrived(ref, at):
        wide = ref[:, pl.ds(0, square), :].astype(F32).reshape(strips, rows, rows, ref.shape[2])
        first = at // cols
        parts = [wide[:, r].reshape(cols, ref.shape[2]) for r in range(first, first + chunk)]
        return jnp.concatenate(parts, 0).astype(BF16)

    @pl.when(p < pairs - 1)
    def _():
        wait_bytes(above, cross_recv.at[1])
        for at in starts:
            here = pl.ds(at, step)
            both, gp, ga = edges(xd[1, here], arrived(above, at), gb[3, here], w1[1])
            acc[here] += mm(gp, vw[1])
            wacc[1] += weight_sums(gp, ga, both)

    @pl.when(p > 0)
    def _():
        wait_bytes(below, cross_recv.at[0])
        lanes = below.shape[2]
        tile = below[:, pl.ds(square, TILE), :].astype(F32)
        pick = (
            lax.broadcasted_iota(jnp.int32, (rows, lanes), 0)
            == lax.broadcasted_iota(jnp.int32, (rows, lanes), 1)
        ).astype(F32)
        ones = jnp.ones((lanes, lanes), BF16)
        for at in starts:
            here = pl.ds(at, step)
            first = at // cols
            parts = [
                (tile[:, r : r + 1, :] * pick[None]).reshape(cols, lanes)
                for r in range(first, first + chunk)
            ]
            gate = mm(jnp.concatenate(parts, 0).astype(BF16), ones)
            _, gp, _ = edges(arrived(below, at), xd[0, here], gate, w1[1])
            acc[here] += mm(gp, vw[2])

    feat = wacc.shape[2] // 4
    hidden = wacc.shape[1] // 2
    for kind in range(2):
        g = wacc[kind]
        sd = jnp.concatenate((g[:hidden, :feat], g[:hidden, 2 * feat : 3 * feat]), 1)
        o = g[hidden:, 3 * feat :] - g[hidden:, feat : 2 * feat]
        o = jnp.concatenate((o[: hidden // 2], o[hidden // 2 :]), 1)
        part = jnp.concatenate((sd, o), 0).astype(BF16)
        wpart[pl.ds(kind * (owners // 2), owners // 2)] = part.reshape(owners // 2, TILE, part.shape[1])

    @pl.loop(1, devices)
    def _(k):
        target, to = place(k)

        @pl.when(target < owners)
        def _():
            send(wpart.at[target], wrecv.at[devices - 1 - k], red_send.at[0], red_recv.at[0], to)

    @pl.when(flat < owners)
    def _():
        wait_bytes(wrecv, red_recv.at[0])
        total = jnp.sum(wrecv[...].astype(F32), 0) + wpart[flat].astype(F32)
        wres[flat] = total.astype(BF16)

        @pl.loop(1, devices)
        def _(k):
            send(wres.at[flat], wres.at[flat], red_send.at[1], red_recv.at[1], place(k)[1])

        few = pl.ds(0, owners - 1)
        wait_bytes(wres.at[few], red_recv.at[1])
        wait_bytes(wpart.at[few], red_send.at[0])
        wait_bytes(wrecv, red_send.at[1])

    @pl.when(flat >= owners)
    def _():
        wait_bytes(wres, red_recv.at[1])
        wait_bytes(wpart, red_send.at[0])

    @pl.when(p < pairs - 1)
    def _():
        wait_bytes(s_up, cross_send.at[0])

    @pl.when(p > 0)
    def _():
        wait_bytes(s_dn, cross_send.at[1])

    w_sum[...] = wres[...].astype(F32)


def on_device(nodes, upstream, usage, blockage, capacity, w_src, w_dst, w_out):
    pair = lax.axis_index("lyr")
    strip_at = lax.axis_index("strip")
    pairs = lax.axis_size("lyr")
    strips = lax.axis_size("strip")
    _, layers, feat, rows, cols = nodes.shape
    hidden = w_src.shape[1]
    cells = rows * cols
    damp = lax.rsqrt(1.0 + usage[0].astype(F32))[:, None]
    feats = (nodes[0].astype(F32) * damp).astype(BF16)
    both = jnp.concatenate((feats, upstream[0]), 1)
    xd = jnp.transpose(both, (0, 2, 3, 1)).reshape(layers, cells, 2 * feat)
    turned = jnp.transpose(both, (0, 3, 2, 1)).reshape(layers, strips, rows * rows, 2 * feat)
    gates = (1 - blockage[0]).astype(F32) * capacity[0].astype(F32) * 0.25
    in_rows = (strip_at * rows + jnp.arange(rows) < cols - 1).astype(F32)[:, None]
    in_cols = (jnp.arange(cols) < cols - 1).astype(F32)[None, :]
    first = pair % 2 == 0
    inside = jnp.stack((jnp.where(first, in_rows, in_cols), jnp.where(first, in_cols, in_rows)))
    four = jnp.concatenate((gates[:, 0] * inside, gates[:, 1]), 0).astype(BF16)
    gb = jnp.broadcast_to(four.reshape(4, cells, 1), (4, cells, 2 * feat))
    tile = jnp.transpose(gates[1, 1].astype(BF16).reshape(rows, strips, rows), (1, 2, 0))
    tile = jnp.pad(tile, ((0, 0), (0, TILE - rows), (0, 2 * feat - rows)))
    s_up = jnp.concatenate((turned[1], tile), 1)
    s_dn = turned[0]

    zero = jnp.zeros((2, feat, hidden), BF16)
    w1 = jnp.concatenate(
        (
            jnp.concatenate((jnp.swapaxes(w_src, 1, 2), zero), 2),
            jnp.concatenate((zero, -w_out), 2),
            jnp.concatenate((jnp.swapaxes(w_dst, 1, 2), zero), 2),
            jnp.concatenate((zero, w_out), 2),
        ),
        1,
    )
    blank = jnp.zeros((2 * hidden, feat), BF16)
    planar = jnp.concatenate((w_src[0], w_dst[0]), 0)
    pw = jnp.stack((jnp.concatenate((planar, blank), 1), jnp.concatenate((blank, planar), 1)))
    none = jnp.zeros((hidden, feat), BF16)
    vw = jnp.stack(
        (
            jnp.concatenate((w_src[1], w_dst[1]), 1),
            jnp.concatenate((none, w_src[1]), 1),
            jnp.concatenate((w_dst[1], none), 1),
        )
    )
    lanes = 2 * feat
    owners = 2 * 3 * hidden * feat // (TILE * lanes)
    devices = pairs * strips
    chunk = max(1, min(rows, 1024 // cols))
    vmem = pl.BlockSpec(memory_space=pltpu.VMEM)
    acc, w_sum = pl.pallas_call(
        functools.partial(kernel, pairs, strips, rows, cols, chunk),
        out_shape=(
            jax.ShapeDtypeStruct((cells, lanes), F32),
            jax.ShapeDtypeStruct((owners, TILE, lanes), F32),
        ),
        in_specs=[vmem] * 7,
        out_specs=(vmem, vmem),
        scratch_shapes=[
            pltpu.VMEM((cols, lanes), BF16),
            pltpu.VMEM((cols, lanes), BF16),
            pltpu.VMEM((cols, lanes), BF16),
            pltpu.VMEM((strips, rows * rows + TILE, lanes), BF16),
            pltpu.VMEM((strips, rows * rows, lanes), BF16),
            pltpu.VMEM((cells + cols, hidden), BF16),
            pltpu.VMEM((2, 2 * hidden, 4 * feat), F32),
            pltpu.VMEM((owners, TILE, lanes), BF16),
            pltpu.VMEM((devices - 1, TILE, lanes), BF16),
            pltpu.VMEM((owners, TILE, lanes), BF16),
            pltpu.SemaphoreType.DMA((3,)),
            pltpu.SemaphoreType.DMA((3,)),
            pltpu.SemaphoreType.DMA((2,)),
            pltpu.SemaphoreType.DMA((2,)),
            pltpu.SemaphoreType.DMA((2,)),
            pltpu.SemaphoreType.DMA((2,)),
        ],
        compiler_params=pltpu.CompilerParams(
            collective_id=0, has_side_effects=True, vmem_limit_bytes=48 * 1024 * 1024
        ),
    )(xd, s_up, s_dn, gb, w1, pw, vw)

    node_sum = jnp.transpose(acc.reshape(rows, cols, layers, feat), (2, 3, 0, 1))
    grad_nodes = (upstream[0].astype(F32) + damp * node_sum).astype(BF16)[None]
    scale = 1.0 / math.sqrt(2 * pairs * cols * cols)
    w_sum = w_sum.reshape(2, 3 * hidden // 2, lanes) * scale
    g_src = w_sum[:, :hidden, :feat]
    g_dst = w_sum[:, :hidden, feat:]
    out = w_sum[:, hidden:]
    g_out = jnp.swapaxes(jnp.concatenate((out[:, :, :feat], out[:, :, feat:]), 1), 1, 2)
    return grad_nodes, g_src, g_dst, g_out


def solution(mesh):
    placed = (
        P("lyr", None, None, "strip", None),
        P("lyr", None, None, "strip", None),
        P("lyr", None, "strip", None),
        P("lyr", None, None, "strip", None),
        P("lyr", None, None, "strip", None),
        P(),
        P(),
        P(),
    )
    return jax.shard_map(
        on_device,
        mesh=mesh,
        in_specs=placed,
        out_specs=(P("lyr", None, None, "strip", None), P(), P(), P()),
        check_vma=False,
    )
```

```python
import functools
import math

import jax
import jax.numpy as jnp
from jax import lax
from jax.experimental import pallas as pl
from jax.experimental.pallas import tpu as pltpu
from jax.sharding import PartitionSpec as P

MESH = pl.DeviceIdType.MESH
F32 = jnp.float32
BF16 = jnp.bfloat16
TILE = 16


def mm(a, b):
    return jnp.dot(a, b, preferred_element_type=F32)


def edges(xu, xv, gate, w):
    both = jnp.concatenate((xu, xv), 1)
    y = mm(both, w)
    half = w.shape[1] // 2
    pre, raw = y[:, :half], y[:, half:]
    s = 0.5 * jnp.tanh(0.5 * pre) + 0.5
    act = pre * s
    slope = s + act * (1.0 - s)
    gate = gate.astype(F32)
    return both, (gate * raw * slope).astype(BF16), (gate * act).astype(BF16)


def weight_sums(gp, ga, both):
    left = jnp.concatenate((gp, ga), 1)
    return lax.dot_general(left, both, (((0,), (0,)), ((), ())), preferred_element_type=F32)


def kernel(
    pairs, strips, rows, cols, chunk,
    nodes, up, usage, blockage, capacity, w_src, w_dst, w_out,
    acc, w_sum,
    xd, s_up, s_dn, gb, w1, pw, vw,
    nv, uv, usv, bv, cv, wsv, wdv, wov, t_rows, q_rows, in_sems,
    prev_x, next_x, prev_g, below, above, gps, wacc, wpart, wrecv, wres,
    halo_send, halo_recv, cross_send, cross_recv, red_send, red_recv,
):
    p = lax.axis_index("lyr")
    s = lax.axis_index("strip")
    devices = pairs * strips
    flat = p * strips + s
    owners = wpart.shape[0]
    cells = rows * cols
    step = chunk * cols
    square = rows * rows

    def place(k):
        target = lax.rem(flat + k, devices)
        return target, (lax.div(target, strips), lax.rem(target, strips))

    barrier = pltpu.get_barrier_semaphore()

    @pl.loop(1, devices)
    def _(k):
        pl.semaphore_signal(barrier, inc=1, device_id=place(k)[1], device_id_type=MESH)

    stage(
        pairs, strips,
        nodes, up, usage, blockage, capacity, w_src, w_dst, w_out,
        xd, s_up, s_dn, gb, w1, pw, vw,
        nv, uv, usv, bv, cv, wsv, wdv, wov, t_rows, q_rows, in_sems,
    )
    pl.semaphore_wait(barrier, devices - 1)

    jr = lax.rem(p, 2)
    jc = 1 - jr

    def send(src, dst, a, b, to):
        copy = pltpu.make_async_remote_copy(
            src_ref=src, dst_ref=dst, send_sem=a, recv_sem=b, device_id=to, device_id_type=MESH
        )
        copy.start()
        return copy

    def wait_bytes(ref, sem):
        pltpu.make_async_copy(ref, ref, sem).wait()

    after = (p, lax.rem(s + 1, strips))
    before = (p, lax.rem(s + strips - 1, strips))
    last = pl.ds(cells - cols, cols)
    halos = (
        send(xd.at[jr, pl.ds(0, cols)], next_x, halo_send.at[0], halo_recv.at[0], before),
        send(xd.at[jr, last], prev_x, halo_send.at[1], halo_recv.at[1], after),
        send(gb.at[jr, last], prev_g, halo_send.at[2], halo_recv.at[2], after),
    )

    @pl.loop(0, strips)
    def _(k):
        t = lax.rem(s + k, strips)

        @pl.when(p < pairs - 1)
        def _():
            send(s_up.at[t], below.at[s], cross_send.at[0], cross_recv.at[0], (p + 1, t))

        @pl.when(p > 0)
        def _():
            send(s_dn.at[t], above.at[s], cross_send.at[1], cross_recv.at[1], (p - 1, t))

    starts = range(0, cells, step)
    for at in starts:
        here = pl.ds(at, step)
        both, gp, ga = edges(xd[0, here], xd[1, here], gb[2, here], w1[1])
        acc[here] = mm(gp, vw[0])
        sums = weight_sums(gp, ga, both)
        wacc[1] = sums if at == 0 else wacc[1] + sums
    for at in starts:
        here = pl.ds(at, step)
        xu = xd[jc, here]
        wide = xu.astype(F32)
        xv = jnp.concatenate((wide[1:], wide[:1]), 0).astype(BF16)
        both, gp, ga = edges(xu, xv, gb[jc, here], w1[0])
        wide = gp.astype(F32)
        turned = jnp.concatenate((wide[-1:], wide[:-1]), 0).astype(BF16)
        acc[here] += mm(jnp.concatenate((gp, turned), 1), pw[jc])
        sums = weight_sums(gp, ga, both)
        wacc[0] = sums if at == 0 else wacc[0] + sums
    for copy in halos:
        copy.wait()
    _, gp, _ = edges(prev_x[...], xd[jr, pl.ds(0, cols)], prev_g[...], w1[0])
    gps[pl.ds(0, cols)] = gp
    for at in starts:
        here = pl.ds(at, step)
        if at + step < cells:
            xv = xd[jr, pl.ds(at + cols, step)]
        elif step > cols:
            xv = jnp.concatenate((xd[jr, pl.ds(at + cols, step - cols)], next_x[...]), 0)
        else:
            xv = next_x[...]
        both, gp, ga = edges(xd[jr, here], xv, gb[jr, here], w1[0])
        gps[pl.ds(at + cols, step)] = gp
        acc[here] += mm(jnp.concatenate((gp, gps[here]), 1), pw[jr])
        wacc[0] += weight_sums(gp, ga, both)

    feat = wacc.shape[2] // 4
    hidden = wacc.shape[1] // 2

    def reduce_out(kind):
        half = owners // 2
        g = wacc[kind]
        sd = jnp.concatenate((g[:hidden, :feat], g[:hidden, 2 * feat : 3 * feat]), 1)
        o = g[hidden:, 3 * feat :] - g[hidden:, feat : 2 * feat]
        o = jnp.concatenate((o[: hidden // 2], o[hidden // 2 :]), 1)
        part = jnp.concatenate((sd, o), 0).astype(BF16)
        wpart[pl.ds(kind * half, half)] = part.reshape(half, TILE, part.shape[1])

        @pl.loop(1, devices)
        def _(k):
            target, to = place(k)

            @pl.when((target >= kind * half) & (target < (kind + 1) * half))
            def _():
                send(wpart.at[target], wrecv.at[devices - 1 - k], red_send.at[0], red_recv.at[0], to)

    reduce_out(0)

    def arrived(ref, at):
        wide = ref[:, pl.ds(0, square), :].astype(F32).reshape(strips, rows, rows, ref.shape[2])
        first = at // cols
        parts = [wide[:, r].reshape(cols, ref.shape[2]) for r in range(first, first + chunk)]
        return jnp.concatenate(parts, 0).astype(BF16)

    @pl.when(p < pairs - 1)
    def _():
        wait_bytes(above, cross_recv.at[1])
        for at in starts:
            here = pl.ds(at, step)
            both, gp, ga = edges(xd[1, here], arrived(above, at), gb[3, here], w1[1])
            acc[here] += mm(gp, vw[1])
            wacc[1] += weight_sums(gp, ga, both)

    @pl.when(p > 0)
    def _():
        wait_bytes(below, cross_recv.at[0])
        lanes = below.shape[2]
        tile = below[:, pl.ds(square, TILE), :].astype(F32)
        pick = (
            lax.broadcasted_iota(jnp.int32, (rows, lanes), 0)
            == lax.broadcasted_iota(jnp.int32, (rows, lanes), 1)
        ).astype(F32)
        ones = jnp.ones((lanes, lanes), BF16)
        for at in starts:
            here = pl.ds(at, step)
            first = at // cols
            parts = [
                (tile[:, r : r + 1, :] * pick[None]).reshape(cols, lanes)
                for r in range(first, first + chunk)
            ]
            gate = mm(jnp.concatenate(parts, 0).astype(BF16), ones)
            _, gp, _ = edges(arrived(below, at), xd[0, here], gate, w1[1])
            acc[here] += mm(gp, vw[2])

    reduce_out(1)

    @pl.when(flat < owners)
    def _():
        wait_bytes(wrecv, red_recv.at[0])
        total = jnp.sum(wrecv[...].astype(F32), 0) + wpart[flat].astype(F32)
        wres[flat] = total.astype(BF16)

        @pl.loop(1, devices)
        def _(k):
            send(wres.at[flat], wres.at[flat], red_send.at[1], red_recv.at[1], place(k)[1])

        few = pl.ds(0, owners - 1)
        wait_bytes(wres.at[few], red_recv.at[1])
        wait_bytes(wpart.at[few], red_send.at[0])
        wait_bytes(wrecv, red_send.at[1])

    @pl.when(flat >= owners)
    def _():
        wait_bytes(wres, red_recv.at[1])
        wait_bytes(wpart, red_send.at[0])

    @pl.when(p < pairs - 1)
    def _():
        wait_bytes(s_up, cross_send.at[0])

    @pl.when(p > 0)
    def _():
        wait_bytes(s_dn, cross_send.at[1])

    w_sum[...] = wres[...].astype(F32)


LANES = 128


def fetch(pairs_of_refs, sems):
    copies = [pltpu.make_async_copy(a, b, sems.at[i]) for i, (a, b) in enumerate(pairs_of_refs)]
    for copy in copies:
        copy.start()
    for copy in copies:
        copy.wait()


def stage(
    pairs, strips,
    nodes, up, usage, blockage, capacity, w_src, w_dst, w_out,
    xd, s_up, s_dn, gb, w1, pw, vw,
    nv, uv, usv, bv, cv, wsv, wdv, wov, t, q, sems,
):
    p = lax.axis_index("lyr")
    s = lax.axis_index("strip")
    fetch(
        (
            (nodes, nv), (up, uv), (usage, usv), (blockage, bv), (capacity, cv),
            (w_src, wsv), (w_dst, wdv), (w_out, wov),
        ),
        sems,
    )
    _, layers, feat, rows, cols = nv.shape
    lanes = 2 * feat
    half = feat * rows
    blocks = cols // LANES
    damp = lax.rsqrt(1.0 + usv[0].astype(F32))
    for j in range(layers):
        x = (nv[0, j].astype(F32) * damp[j][None]).astype(BF16).astype(F32)
        d = uv[0, j].astype(F32)
        for b in range(blocks):
            cut = slice(b * LANES, (b + 1) * LANES)
            t[b, pl.ds(0, half)] = x[:, :, cut].reshape(half, LANES)
            t[b, pl.ds(half, half)] = d[:, :, cut].reshape(half, LANES)
        for r in range(rows):
            for b in range(blocks):
                m = t[b, pl.ds(r, lanes, stride=rows), :]
                xd[j, pl.ds(r * cols + b * LANES, LANES)] = m.T.astype(BF16)

    def spread(j, out):
        for r in range(rows):
            q[pl.ds(r, cols, stride=rows), :] = xd[j, pl.ds(r * cols, cols)].astype(F32)
        out[:, pl.ds(0, rows * rows), :] = q[...].astype(BF16).reshape(strips, rows * rows, lanes)

    @pl.when(p > 0)
    def _():
        spread(0, s_dn)

    gates = (1 - bv[0]).astype(F32) * cv[0].astype(F32) * 0.25

    @pl.when(p < pairs - 1)
    def _():
        spread(1, s_up)
        per = LANES // rows
        for b in range(blocks):
            g = gates[1, 1][:, b * LANES : (b + 1) * LANES]
            g = jnp.concatenate((g, jnp.zeros((LANES - rows, LANES), F32)), 0).T.reshape(per, rows, LANES)
            g = jnp.concatenate((g, jnp.zeros((per, TILE - rows, LANES), F32)), 1)
            s_up[pl.ds(b * per, per), pl.ds(rows * rows, TILE), :] = g.astype(BF16)

    row_ids = s * rows + lax.broadcasted_iota(jnp.int32, (rows, cols), 0)
    in_rows = (row_ids < cols - 1).astype(F32)
    in_cols = (lax.broadcasted_iota(jnp.int32, (rows, cols), 1) < cols - 1).astype(F32)
    odd = lax.rem(p, 2).astype(F32)
    low = (1.0 - odd) * in_rows + odd * in_cols
    high = odd * in_rows + (1.0 - odd) * in_cols
    four = (gates[0, 0] * low, gates[1, 0] * high, gates[0, 1], gates[1, 1])
    eye = (
        lax.broadcasted_iota(jnp.int32, (LANES, LANES), 0)
        == lax.broadcasted_iota(jnp.int32, (LANES, LANES), 1)
    ).astype(F32)
    ones = jnp.ones((LANES, lanes), BF16)
    for k, g in enumerate(four):
        parts = [
            (eye * g[r : r + 1, b * LANES : (b + 1) * LANES]).astype(BF16)
            for r in range(rows)
            for b in range(blocks)
        ]
        gb[k] = mm(jnp.concatenate(parts, 0), ones).astype(BF16)

    hidden = wsv.shape[2]
    zero = jnp.zeros((feat, hidden), BF16)
    for k in range(2):
        wo = wov[k]
        less = (-wo.astype(F32)).astype(BF16)
        w1[k, pl.ds(0, feat)] = jnp.concatenate((wsv[k], zero), 1)
        w1[k, pl.ds(feat, feat)] = jnp.concatenate((zero, less), 1)
        w1[k, pl.ds(2 * feat, feat)] = jnp.concatenate((wdv[k], zero), 1)
        w1[k, pl.ds(3 * feat, feat)] = jnp.concatenate((zero, wo), 1)
    none = jnp.zeros((hidden, feat), BF16)
    src, dst = [[v[k].astype(F32).T.astype(BF16) for k in range(2)] for v in (wsv, wdv)]
    for i, w in enumerate((src, dst)):
        here = pl.ds(i * hidden, hidden)
        pw[0, here] = jnp.concatenate((w[0], none), 1)
        pw[1, here] = jnp.concatenate((none, w[0]), 1)
    vw[0] = jnp.concatenate((src[1], dst[1]), 1)
    vw[1] = jnp.concatenate((none, src[1]), 1)
    vw[2] = jnp.concatenate((dst[1], none), 1)


def finish(scale, acc_in, w_in, up, usage, gn, gs, gd, go, acc, w_sum, uv, usv, t, sems):
    fetch(((acc_in, acc), (w_in, w_sum), (up, uv), (usage, usv)), sems)
    _, layers, feat, rows, cols = uv.shape
    lanes = 2 * feat
    half = feat * rows
    blocks = cols // LANES
    for b in range(blocks):
        for r in range(rows):
            t[b, pl.ds(r, lanes, stride=rows), :] = acc[pl.ds(r * cols + b * LANES, LANES)].T
    damp = lax.rsqrt(1.0 + usv[0].astype(F32))
    for j in range(layers):
        for b in range(blocks):
            cut = pl.ds(b * LANES, LANES)
            ns = t[b, pl.ds(j * half, half)].reshape(feat, rows, LANES)
            scaled = damp[j][None, :, b * LANES : (b + 1) * LANES] * ns
            gn[0, j, :, :, cut] = (uv[0, j, :, :, cut].astype(F32) + scaled).astype(BF16)
    hidden = gs.shape[2]
    w = w_sum[...].reshape(2, 3 * hidden // 2, lanes) * scale
    for k in range(2):
        sd = w[k, :hidden].T
        gs[k] = sd[:feat]
        gd[k] = sd[feat:]
        o = w[k, hidden:]
        go[k] = jnp.concatenate((o[:, :feat], o[:, feat:]), 0).T


def on_device(nodes, upstream, usage, blockage, capacity, w_src, w_dst, w_out):
    pairs = lax.axis_size("lyr")
    strips = lax.axis_size("strip")
    _, layers, feat, rows, cols = nodes.shape
    hidden = w_src.shape[1]
    cells = rows * cols
    lanes = 2 * feat
    owners = 2 * 3 * hidden * feat // (TILE * lanes)
    devices = pairs * strips
    chunk = max(1, min(rows, 1024 // cols))
    vmem = pl.BlockSpec(memory_space=pltpu.VMEM)
    hbm = pl.BlockSpec(memory_space=pltpu.HBM)
    params = pltpu.CompilerParams(vmem_limit_bytes=63 * 1024 * 1024)
    given = (nodes, upstream, usage, blockage, capacity)
    given += (jnp.swapaxes(w_src, 1, 2), jnp.swapaxes(w_dst, 1, 2), w_out)

    def shape(dims, kind=BF16):
        return jax.ShapeDtypeStruct(dims, kind)

    acc, w_sum = pl.pallas_call(
        functools.partial(kernel, pairs, strips, rows, cols, chunk),
        out_shape=(
            jax.ShapeDtypeStruct((cells, lanes), F32),
            jax.ShapeDtypeStruct((owners, TILE, lanes), F32),
        ),
        in_specs=[hbm] * 8,
        out_specs=(vmem, vmem),
        scratch_shapes=[
            pltpu.VMEM((layers, cells, lanes), BF16),
            pltpu.VMEM((strips, rows * rows + TILE, lanes), BF16),
            pltpu.VMEM((strips, rows * rows, lanes), BF16),
            pltpu.VMEM((4, cells, lanes), BF16),
            pltpu.VMEM((2, 4 * feat, 2 * hidden), BF16),
            pltpu.VMEM((2, 2 * hidden, lanes), BF16),
            pltpu.VMEM((3, hidden, lanes), BF16),
        ]
        + [pltpu.VMEM(a.shape, a.dtype) for a in given]
        + [
            pltpu.VMEM((cols // LANES, lanes * rows, LANES), F32),
            pltpu.VMEM((cells, lanes), F32),
            pltpu.SemaphoreType.DMA((8,)),
            pltpu.VMEM((cols, lanes), BF16),
            pltpu.VMEM((cols, lanes), BF16),
            pltpu.VMEM((cols, lanes), BF16),
            pltpu.VMEM((strips, rows * rows + TILE, lanes), BF16),
            pltpu.VMEM((strips, rows * rows, lanes), BF16),
            pltpu.VMEM((cells + cols, hidden), BF16),
            pltpu.VMEM((2, 2 * hidden, 4 * feat), F32),
            pltpu.VMEM((owners, TILE, lanes), BF16),
            pltpu.VMEM((devices - 1, TILE, lanes), BF16),
            pltpu.VMEM((owners, TILE, lanes), BF16),
            pltpu.SemaphoreType.DMA((3,)),
            pltpu.SemaphoreType.DMA((3,)),
            pltpu.SemaphoreType.DMA((2,)),
            pltpu.SemaphoreType.DMA((2,)),
            pltpu.SemaphoreType.DMA((2,)),
            pltpu.SemaphoreType.DMA((2,)),
        ],
        compiler_params=pltpu.CompilerParams(
            collective_id=0, has_side_effects=True, vmem_limit_bytes=63 * 1024 * 1024
        ),
    )(*given)

    scale = 1.0 / math.sqrt(2 * pairs * cols * cols)
    gn, gs, gd, go = pl.pallas_call(
        functools.partial(finish, scale),
        out_shape=(
            shape(nodes.shape),
            shape((2, feat, hidden), F32),
            shape((2, feat, hidden), F32),
            shape(w_out.shape, F32),
        ),
        in_specs=[hbm] * 4,
        out_specs=(vmem,) * 4,
        scratch_shapes=[
            pltpu.VMEM(acc.shape, acc.dtype),
            pltpu.VMEM(w_sum.shape, w_sum.dtype),
            pltpu.VMEM(upstream.shape, upstream.dtype),
            pltpu.VMEM(usage.shape, usage.dtype),
            pltpu.VMEM((cols // LANES, lanes * rows, LANES), F32),
            pltpu.SemaphoreType.DMA((4,)),
        ],
        compiler_params=params,
    )(acc, w_sum, upstream, usage)
    return gn, jnp.swapaxes(gs, 1, 2), jnp.swapaxes(gd, 1, 2), go


def solution(mesh):
    placed = (
        P("lyr", None, None, "strip", None),
        P("lyr", None, None, "strip", None),
        P("lyr", None, "strip", None),
        P("lyr", None, None, "strip", None),
        P("lyr", None, None, "strip", None),
        P(),
        P(),
        P(),
    )
    return jax.shard_map(
        on_device,
        mesh=mesh,
        in_specs=placed,
        out_specs=(P("lyr", None, None, "strip", None), P(), P(), P()),
        check_vma=False,
    )
```

```python
import functools
import math

import jax
import jax.numpy as jnp
from jax import lax
from jax.experimental import pallas as pl
from jax.experimental.pallas import tpu as pltpu
from jax.sharding import PartitionSpec as P

MESH = pl.DeviceIdType.MESH
F32 = jnp.float32
BF16 = jnp.bfloat16
TILE = 16


def mm(a, b):
    return jnp.dot(a, b, preferred_element_type=F32)


def edges(xu, xv, gate, w):
    both = jnp.concatenate((xu, xv), 1)
    y = mm(both, w)
    half = w.shape[1] // 2
    pre, raw = y[:, :half], y[:, half:]
    s = 0.5 * jnp.tanh(0.5 * pre) + 0.5
    act = pre * s
    slope = s + act * (1.0 - s)
    gate = gate.astype(F32)
    return both, (gate * raw * slope).astype(BF16), (gate * act).astype(BF16)


def weight_sums(gp, ga, both):
    left = jnp.concatenate((gp, ga), 1)
    return lax.dot_general(left, both, (((0,), (0,)), ((), ())), preferred_element_type=F32)


def kernel(
    pairs, strips, rows, cols, chunk,
    nodes, up, usage, blockage, capacity, w_src, w_dst, w_out,
    gn, w_sum,
    acc, gv,
    xd, s_up, s_dn, gb, w1, pw, vw,
    nv, uv, usv, bv, cv, wsv, wdv, wov, t_rows, q_rows, in_sems,
    prev_x, next_x, prev_g, below, above, gps, wacc, wpart, wrecv, wres,
    halo_send, halo_recv, cross_send, cross_recv, red_send, red_recv,
):
    p = lax.axis_index("lyr")
    s = lax.axis_index("strip")
    devices = pairs * strips
    flat = p * strips + s
    owners = wpart.shape[0]
    cells = rows * cols
    step = chunk * cols
    square = rows * rows

    def place(k):
        target = lax.rem(flat + k, devices)
        return target, (lax.div(target, strips), lax.rem(target, strips))

    barrier = pltpu.get_barrier_semaphore()

    jr = lax.rem(p, 2)
    jc = 1 - jr

    def send(src, dst, a, b, to):
        copy = pltpu.make_async_remote_copy(
            src_ref=src, dst_ref=dst, send_sem=a, recv_sem=b, device_id=to, device_id_type=MESH
        )
        copy.start()
        return copy

    def wait_bytes(ref, sem):
        pltpu.make_async_copy(ref, ref, sem).wait()

    def greet():
        @pl.loop(1, devices)
        def _(k):
            pl.semaphore_signal(barrier, inc=1, device_id=place(k)[1], device_id_type=MESH)

    def ready():
        pl.semaphore_wait(barrier, devices - 1)

    def cross(j):
        @pl.when((j == 1) & (p < pairs - 1))
        def _():
            @pl.loop(0, strips)
            def _(k):
                t = lax.rem(s + k, strips)
                send(s_up.at[t], below.at[s], cross_send.at[0], cross_recv.at[0], (p + 1, t))

        @pl.when((j == 0) & (p > 0))
        def _():
            @pl.loop(0, strips)
            def _(k):
                t = lax.rem(s + k, strips)
                send(s_dn.at[t], above.at[s], cross_send.at[1], cross_recv.at[1], (p - 1, t))

    stage_cells(
        pairs, strips, greet, ready, cross,
        nodes, up, usage, blockage, capacity, w_src, w_dst, w_out,
        xd, s_up, s_dn,
        nv, uv, usv, bv, cv, wsv, wdv, wov, t_rows, q_rows, in_sems,
    )
    after = (p, lax.rem(s + 1, strips))
    before = (p, lax.rem(s + strips - 1, strips))
    last = pl.ds(cells - cols, cols)
    halos = [
        send(xd.at[jr, pl.ds(0, cols)], next_x, halo_send.at[0], halo_recv.at[0], before),
        send(xd.at[jr, last], prev_x, halo_send.at[1], halo_recv.at[1], after),
    ]
    stage_rest(gb, w1, pw, vw, bv, cv, wsv, wdv, wov)
    halos.append(send(gb.at[jr, last], prev_g, halo_send.at[2], halo_recv.at[2], after))

    starts = range(0, cells, step)
    for at in starts:
        here = pl.ds(at, step)
        both, gp, ga = edges(xd[0, here], xd[1, here], gb[2, here], w1[1])
        acc[here] = mm(gp, vw[0])
        sums = weight_sums(gp, ga, both)
        wacc[1] = sums if at == 0 else wacc[1] + sums
    for at in starts:
        here = pl.ds(at, step)
        xu = xd[jc, here]
        wide = xu.astype(F32)
        xv = jnp.concatenate((wide[1:], wide[:1]), 0).astype(BF16)
        both, gp, ga = edges(xu, xv, gb[jc, here], w1[0])
        wide = gp.astype(F32)
        turned = jnp.concatenate((wide[-1:], wide[:-1]), 0).astype(BF16)
        acc[here] += mm(jnp.concatenate((gp, turned), 1), pw[jc])
        sums = weight_sums(gp, ga, both)
        wacc[0] = sums if at == 0 else wacc[0] + sums
    for copy in halos:
        copy.wait()
    _, gp, _ = edges(prev_x[...], xd[jr, pl.ds(0, cols)], prev_g[...], w1[0])
    gps[pl.ds(0, cols)] = gp
    for at in starts:
        here = pl.ds(at, step)
        if at + step < cells:
            xv = xd[jr, pl.ds(at + cols, step)]
        elif step > cols:
            xv = jnp.concatenate((xd[jr, pl.ds(at + cols, step - cols)], next_x[...]), 0)
        else:
            xv = next_x[...]
        both, gp, ga = edges(xd[jr, here], xv, gb[jr, here], w1[0])
        gps[pl.ds(at + cols, step)] = gp
        acc[here] += mm(jnp.concatenate((gp, gps[here]), 1), pw[jr])
        wacc[0] += weight_sums(gp, ga, both)

    feat = wacc.shape[2] // 4
    hidden = wacc.shape[1] // 2

    def reduce_out(kind):
        half = owners // 2
        g = wacc[kind]
        sd = jnp.concatenate((g[:hidden, :feat], g[:hidden, 2 * feat : 3 * feat]), 1)
        o = g[hidden:, 3 * feat :] - g[hidden:, feat : 2 * feat]
        o = jnp.concatenate((o[: hidden // 2], o[hidden // 2 :]), 1)
        part = jnp.concatenate((sd, o), 0).astype(BF16)
        wpart[pl.ds(kind * half, half)] = part.reshape(half, TILE, part.shape[1])

        for i in range(half):
            target = kind * half + lax.rem(flat + i, half)

            @pl.when(target != flat)
            def _(target=target):
                to = (lax.div(target, strips), lax.rem(target, strips))
                slot = lax.rem(flat - target + devices, devices) - 1
                send(wpart.at[target], wrecv.at[slot], red_send.at[0], red_recv.at[0], to)

    reduce_out(0)

    def arrived(ref, at):
        wide = ref[:, pl.ds(0, square), :].astype(F32).reshape(strips, rows, rows, ref.shape[2])
        first = at // cols
        parts = [wide[:, r].reshape(cols, ref.shape[2]) for r in range(first, first + chunk)]
        return jnp.concatenate(parts, 0).astype(BF16)

    @pl.when(p < pairs - 1)
    def _():
        wait_bytes(above, cross_recv.at[1])
        for at in starts:
            here = pl.ds(at, step)
            both, gp, ga = edges(xd[1, here], arrived(above, at), gb[3, here], w1[1])
            acc[here] += mm(gp, vw[1])
            wacc[1] += weight_sums(gp, ga, both)

    @pl.when(p > 0)
    def _():
        wait_bytes(below, cross_recv.at[0])
        lanes = below.shape[2]
        tile = below[:, pl.ds(square, TILE), :].astype(F32)
        pick = (
            lax.broadcasted_iota(jnp.int32, (rows, lanes), 0)
            == lax.broadcasted_iota(jnp.int32, (rows, lanes), 1)
        ).astype(F32)
        ones = jnp.ones((lanes, lanes), BF16)
        for at in starts:
            here = pl.ds(at, step)
            first = at // cols
            parts = [
                (tile[:, r : r + 1, :] * pick[None]).reshape(cols, lanes)
                for r in range(first, first + chunk)
            ]
            gate = mm(jnp.concatenate(parts, 0).astype(BF16), ones)
            _, gp, _ = edges(arrived(below, at), xd[0, here], gate, w1[1])
            acc[here] += mm(gp, vw[2])

    reduce_out(1)

    half = feat * rows
    for b in range(cols // LANES):
        for r in range(rows):
            tile = acc[pl.ds(r * cols + b * LANES, LANES)].T
            t_rows[b, pl.ds(r, 2 * feat, stride=rows), :] = tile
    for j in range(2):
        damp = lax.rsqrt(1.0 + usv[0, j].astype(F32))
        for b in range(cols // LANES):
            cut = pl.ds(b * LANES, LANES)
            ns = t_rows[b, pl.ds(j * half, half)].reshape(feat, rows, LANES)
            scaled = damp[None, :, b * LANES : (b + 1) * LANES] * ns
            gv[0, j, :, :, cut] = (uv[0, j, :, :, cut].astype(F32) + scaled).astype(BF16)
    out_copy = pltpu.make_async_copy(gv, gn, in_sems.at[0])
    out_copy.start()

    @pl.when(flat < owners)
    def _():
        wait_bytes(wrecv, red_recv.at[0])
        total = jnp.sum(wrecv[...].astype(F32), 0) + wpart[flat].astype(F32)
        wres[flat] = total.astype(BF16)

        @pl.loop(1, devices)
        def _(k):
            send(wres.at[flat], wres.at[flat], red_send.at[1], red_recv.at[1], place(k)[1])

        few = pl.ds(0, owners - 1)
        wait_bytes(wres.at[few], red_recv.at[1])
        wait_bytes(wpart.at[few], red_send.at[0])
        wait_bytes(wrecv, red_send.at[1])

    @pl.when(flat >= owners)
    def _():
        wait_bytes(wres, red_recv.at[1])
        wait_bytes(wpart, red_send.at[0])

    @pl.when(p < pairs - 1)
    def _():
        wait_bytes(s_up, cross_send.at[0])

    @pl.when(p > 0)
    def _():
        wait_bytes(s_dn, cross_send.at[1])

    w_sum[...] = wres[...].astype(F32)
    out_copy.wait()


LANES = 128


def fetch(pairs_of_refs, sems, meanwhile=None):
    copies = [pltpu.make_async_copy(a, b, sems.at[i]) for i, (a, b) in enumerate(pairs_of_refs)]
    for copy in copies:
        copy.start()
    if meanwhile is not None:
        meanwhile()
    for copy in copies:
        copy.wait()


def stage_cells(
    pairs, strips, greet, ready, cross,
    nodes, up, usage, blockage, capacity, w_src, w_dst, w_out,
    xd, s_up, s_dn,
    nv, uv, usv, bv, cv, wsv, wdv, wov, t, q, sems,
):
    p = lax.axis_index("lyr")
    fetch(
        (
            (nodes, nv), (up, uv), (usage, usv), (blockage, bv), (capacity, cv),
            (w_src, wsv), (w_dst, wdv), (w_out, wov),
        ),
        sems,
        greet,
    )
    _, layers, feat, rows, cols = nv.shape
    lanes = 2 * feat
    half = feat * rows
    blocks = cols // LANES
    gates = (1 - bv[0, 1, 1]).astype(F32) * cv[0, 1, 1].astype(F32) * 0.25

    def spread(j, out):
        for r in range(rows):
            q[pl.ds(r, cols, stride=rows), :] = xd[j, pl.ds(r * cols, cols)].astype(F32)
        out[:, pl.ds(0, rows * rows), :] = q[...].astype(BF16).reshape(strips, rows * rows, lanes)

    leading = 1 - lax.rem(p, 2)
    for turn in range(layers):
        j = leading if turn == 0 else 1 - leading
        damp = lax.rsqrt(1.0 + usv[0, j].astype(F32))
        x = (nv[0, j].astype(F32) * damp[None]).astype(BF16).astype(F32)
        d = uv[0, j].astype(F32)
        for b in range(blocks):
            cut = slice(b * LANES, (b + 1) * LANES)
            t[b, pl.ds(0, half)] = x[:, :, cut].reshape(half, LANES)
            t[b, pl.ds(half, half)] = d[:, :, cut].reshape(half, LANES)
        for r in range(rows):
            for b in range(blocks):
                m = t[b, pl.ds(r, lanes, stride=rows), :]
                xd[j, pl.ds(r * cols + b * LANES, LANES)] = m.T.astype(BF16)

        @pl.when((j == 0) & (p > 0))
        def _():
            spread(0, s_dn)

        @pl.when((j == 1) & (p < pairs - 1))
        def _():
            spread(1, s_up)
            per = LANES // rows
            for b in range(blocks):
                g = gates[:, b * LANES : (b + 1) * LANES]
                g = jnp.concatenate((g, jnp.zeros((LANES - rows, LANES), F32)), 0).T
                g = g.reshape(per, rows, LANES)
                g = jnp.concatenate((g, jnp.zeros((per, TILE - rows, LANES), F32)), 1)
                s_up[pl.ds(b * per, per), pl.ds(rows * rows, TILE), :] = g.astype(BF16)

        if turn == 0:
            ready()
        cross(j)


def stage_rest(gb, w1, pw, vw, bv, cv, wsv, wdv, wov):
    p = lax.axis_index("lyr")
    s = lax.axis_index("strip")
    rows, cols = bv.shape[3:]
    feat = wsv.shape[1]
    lanes = 2 * feat
    blocks = cols // LANES
    gates = (1 - bv[0]).astype(F32) * cv[0].astype(F32) * 0.25
    row_ids = s * rows + lax.broadcasted_iota(jnp.int32, (rows, cols), 0)
    in_rows = (row_ids < cols - 1).astype(F32)
    in_cols = (lax.broadcasted_iota(jnp.int32, (rows, cols), 1) < cols - 1).astype(F32)
    odd = lax.rem(p, 2).astype(F32)
    low = (1.0 - odd) * in_rows + odd * in_cols
    high = odd * in_rows + (1.0 - odd) * in_cols
    four = (gates[0, 0] * low, gates[1, 0] * high, gates[0, 1], gates[1, 1])
    eye = (
        lax.broadcasted_iota(jnp.int32, (LANES, LANES), 0)
        == lax.broadcasted_iota(jnp.int32, (LANES, LANES), 1)
    ).astype(F32)
    ones = jnp.ones((LANES, lanes), BF16)
    for k, g in enumerate(four):
        parts = [
            (eye * g[r : r + 1, b * LANES : (b + 1) * LANES]).astype(BF16)
            for r in range(rows)
            for b in range(blocks)
        ]
        gb[k] = mm(jnp.concatenate(parts, 0), ones).astype(BF16)

    hidden = wsv.shape[2]
    zero = jnp.zeros((feat, hidden), BF16)
    for k in range(2):
        wo = wov[k]
        less = (-wo.astype(F32)).astype(BF16)
        w1[k, pl.ds(0, feat)] = jnp.concatenate((wsv[k], zero), 1)
        w1[k, pl.ds(feat, feat)] = jnp.concatenate((zero, less), 1)
        w1[k, pl.ds(2 * feat, feat)] = jnp.concatenate((wdv[k], zero), 1)
        w1[k, pl.ds(3 * feat, feat)] = jnp.concatenate((zero, wo), 1)
    none = jnp.zeros((hidden, feat), BF16)
    src, dst = [[v[k].astype(F32).T.astype(BF16) for k in range(2)] for v in (wsv, wdv)]
    for i, w in enumerate((src, dst)):
        here = pl.ds(i * hidden, hidden)
        pw[0, here] = jnp.concatenate((w[0], none), 1)
        pw[1, here] = jnp.concatenate((none, w[0]), 1)
    vw[0] = jnp.concatenate((src[1], dst[1]), 1)
    vw[1] = jnp.concatenate((none, src[1]), 1)
    vw[2] = jnp.concatenate((dst[1], none), 1)


def finish(scale, gn_in, w_sum, gn, gs, gd, go, sem):
    copy = pltpu.make_async_copy(gn_in, gn, sem)
    copy.start()
    feat = gs.shape[1]
    lanes = 2 * feat
    hidden = gs.shape[2]
    w = w_sum[...].reshape(2, 3 * hidden // 2, lanes) * scale
    for k in range(2):
        sd = w[k, :hidden].T
        gs[k] = sd[:feat]
        gd[k] = sd[feat:]
        o = w[k, hidden:]
        go[k] = jnp.concatenate((o[:, :feat], o[:, feat:]), 0).T
    copy.wait()


def on_device(nodes, upstream, usage, blockage, capacity, w_src, w_dst, w_out):
    pairs = lax.axis_size("lyr")
    strips = lax.axis_size("strip")
    _, layers, feat, rows, cols = nodes.shape
    hidden = w_src.shape[1]
    cells = rows * cols
    lanes = 2 * feat
    owners = 2 * 3 * hidden * feat // (TILE * lanes)
    devices = pairs * strips
    chunk = max(1, min(rows, 1024 // cols))
    vmem = pl.BlockSpec(memory_space=pltpu.VMEM)
    hbm = pl.BlockSpec(memory_space=pltpu.HBM)
    params = pltpu.CompilerParams(vmem_limit_bytes=63 * 1024 * 1024)
    given = (nodes, upstream, usage, blockage, capacity)
    given += (jnp.swapaxes(w_src, 1, 2), jnp.swapaxes(w_dst, 1, 2), w_out)

    def shape(dims, kind=BF16):
        return jax.ShapeDtypeStruct(dims, kind)

    gn, w_sum = pl.pallas_call(
        functools.partial(kernel, pairs, strips, rows, cols, chunk),
        out_shape=(
            shape(nodes.shape),
            jax.ShapeDtypeStruct((owners, TILE, lanes), F32),
        ),
        in_specs=[hbm] * 8,
        out_specs=(hbm, vmem),
        scratch_shapes=[
            pltpu.VMEM((cells, lanes), F32),
            pltpu.VMEM(nodes.shape, BF16),
            pltpu.VMEM((layers, cells, lanes), BF16),
            pltpu.VMEM((strips, rows * rows + TILE, lanes), BF16),
            pltpu.VMEM((strips, rows * rows, lanes), BF16),
            pltpu.VMEM((4, cells, lanes), BF16),
            pltpu.VMEM((2, 4 * feat, 2 * hidden), BF16),
            pltpu.VMEM((2, 2 * hidden, lanes), BF16),
            pltpu.VMEM((3, hidden, lanes), BF16),
        ]
        + [pltpu.VMEM(a.shape, a.dtype) for a in given]
        + [
            pltpu.VMEM((cols // LANES, lanes * rows, LANES), F32),
            pltpu.VMEM((cells, lanes), F32),
            pltpu.SemaphoreType.DMA((8,)),
            pltpu.VMEM((cols, lanes), BF16),
            pltpu.VMEM((cols, lanes), BF16),
            pltpu.VMEM((cols, lanes), BF16),
            pltpu.VMEM((strips, rows * rows + TILE, lanes), BF16),
            pltpu.VMEM((strips, rows * rows, lanes), BF16),
            pltpu.VMEM((cells + cols, hidden), BF16),
            pltpu.VMEM((2, 2 * hidden, 4 * feat), F32),
            pltpu.VMEM((owners, TILE, lanes), BF16),
            pltpu.VMEM((devices - 1, TILE, lanes), BF16),
            pltpu.VMEM((owners, TILE, lanes), BF16),
            pltpu.SemaphoreType.DMA((3,)),
            pltpu.SemaphoreType.DMA((3,)),
            pltpu.SemaphoreType.DMA((2,)),
            pltpu.SemaphoreType.DMA((2,)),
            pltpu.SemaphoreType.DMA((2,)),
            pltpu.SemaphoreType.DMA((2,)),
        ],
        compiler_params=pltpu.CompilerParams(
            collective_id=0, has_side_effects=True, vmem_limit_bytes=63 * 1024 * 1024
        ),
    )(*given)

    scale = 1.0 / math.sqrt(2 * pairs * cols * cols)
    gn, gs, gd, go = pl.pallas_call(
        functools.partial(finish, scale),
        out_shape=(
            shape(nodes.shape),
            shape((2, feat, hidden), F32),
            shape((2, feat, hidden), F32),
            shape(w_out.shape, F32),
        ),
        in_specs=[hbm, vmem],
        out_specs=(hbm, vmem, vmem, vmem),
        scratch_shapes=[pltpu.SemaphoreType.DMA],
        compiler_params=params,
    )(gn, w_sum)
    return gn, jnp.swapaxes(gs, 1, 2), jnp.swapaxes(gd, 1, 2), go


def solution(mesh):
    placed = (
        P("lyr", None, None, "strip", None),
        P("lyr", None, None, "strip", None),
        P("lyr", None, "strip", None),
        P("lyr", None, None, "strip", None),
        P("lyr", None, None, "strip", None),
        P(),
        P(),
        P(),
    )
    return jax.shard_map(
        on_device,
        mesh=mesh,
        in_specs=placed,
        out_specs=(P("lyr", None, None, "strip", None), P(), P(), P()),
        check_vma=False,
    )
```

```python
import functools
import math

import jax
import jax.numpy as jnp
from jax import lax
from jax.experimental import pallas as pl
from jax.experimental.pallas import tpu as pltpu
from jax.sharding import PartitionSpec as P

MESH = pl.DeviceIdType.MESH
F32 = jnp.float32
BF16 = jnp.bfloat16
TILE = 16


def mm(a, b):
    return jnp.dot(a, b, preferred_element_type=F32)


def edges(xu, xv, gate, w):
    both = jnp.concatenate((xu, xv), 1)
    y = mm(both, w)
    half = w.shape[1] // 2
    pre, raw = y[:, :half], y[:, half:]
    s = 0.5 * jnp.tanh(0.5 * pre) + 0.5
    act = pre * s
    slope = s + act * (1.0 - s)
    gate = gate.astype(F32)
    return both, (gate * raw * slope).astype(BF16), (gate * act).astype(BF16)


def weight_sums(gp, ga, both):
    left = jnp.concatenate((gp, ga), 1)
    return lax.dot_general(left, both, (((0,), (0,)), ((), ())), preferred_element_type=F32)


def kernel(
    pairs, strips, rows, cols, chunk,
    nodes, up, usage, blockage, capacity, w_src, w_dst, w_out,
    acc_out, w_sum,
    acc,
    xd, s_up, s_dn, gb, w1, pw, vw,
    nv, uv, usv, bv, cv, wsv, wdv, wov, t_rows, q_rows, in_sems,
    prev_x, next_x, prev_g, below, above, gps, wacc, wpart, wrecv, wres,
    halo_send, halo_recv, cross_send, cross_recv, red_send, red_recv,
):
    p = lax.axis_index("lyr")
    s = lax.axis_index("strip")
    devices = pairs * strips
    flat = p * strips + s
    owners = wpart.shape[0]
    cells = rows * cols
    step = chunk * cols
    square = rows * rows

    def place(k):
        target = lax.rem(flat + k, devices)
        return target, (lax.div(target, strips), lax.rem(target, strips))

    barrier = pltpu.get_barrier_semaphore()

    jr = lax.rem(p, 2)
    jc = 1 - jr

    def send(src, dst, a, b, to):
        copy = pltpu.make_async_remote_copy(
            src_ref=src, dst_ref=dst, send_sem=a, recv_sem=b, device_id=to, device_id_type=MESH
        )
        copy.start()
        return copy

    def wait_bytes(ref, sem):
        pltpu.make_async_copy(ref, ref, sem).wait()

    def greet():
        @pl.loop(1, devices)
        def _(k):
            pl.semaphore_signal(barrier, inc=1, device_id=place(k)[1], device_id_type=MESH)

    def ready():
        pl.semaphore_wait(barrier, devices - 1)

    def cross(j):
        @pl.when((j == 1) & (p < pairs - 1))
        def _():
            @pl.loop(0, strips)
            def _(k):
                t = lax.rem(s + k, strips)
                send(s_up.at[t], below.at[s], cross_send.at[0], cross_recv.at[0], (p + 1, t))

        @pl.when((j == 0) & (p > 0))
        def _():
            @pl.loop(0, strips)
            def _(k):
                t = lax.rem(s + k, strips)
                send(s_dn.at[t], above.at[s], cross_send.at[1], cross_recv.at[1], (p - 1, t))

    stage_cells(
        pairs, strips, greet, ready, cross,
        nodes, up, usage, blockage, capacity, w_src, w_dst, w_out,
        xd, s_up, s_dn,
        nv, uv, usv, bv, cv, wsv, wdv, wov, t_rows, q_rows, in_sems,
    )
    after = (p, lax.rem(s + 1, strips))
    before = (p, lax.rem(s + strips - 1, strips))
    last = pl.ds(cells - cols, cols)
    halos = [
        send(xd.at[jr, pl.ds(0, cols)], next_x, halo_send.at[0], halo_recv.at[0], before),
        send(xd.at[jr, last], prev_x, halo_send.at[1], halo_recv.at[1], after),
    ]
    stage_rest(gb, w1, pw, vw, bv, cv, wsv, wdv, wov)
    halos.append(send(gb.at[jr, last], prev_g, halo_send.at[2], halo_recv.at[2], after))

    starts = range(0, cells, step)
    for at in starts:
        here = pl.ds(at, step)
        both, gp, ga = edges(xd[0, here], xd[1, here], gb[2, here], w1[1])
        acc[here] = mm(gp, vw[0])
        sums = weight_sums(gp, ga, both)
        wacc[1] = sums if at == 0 else wacc[1] + sums
    for at in starts:
        here = pl.ds(at, step)
        xu = xd[jc, here]
        wide = xu.astype(F32)
        xv = jnp.concatenate((wide[1:], wide[:1]), 0).astype(BF16)
        both, gp, ga = edges(xu, xv, gb[jc, here], w1[0])
        wide = gp.astype(F32)
        turned = jnp.concatenate((wide[-1:], wide[:-1]), 0).astype(BF16)
        acc[here] += mm(jnp.concatenate((gp, turned), 1), pw[jc])
        sums = weight_sums(gp, ga, both)
        wacc[0] = sums if at == 0 else wacc[0] + sums
    for copy in halos:
        copy.wait()
    _, gp, _ = edges(prev_x[...], xd[jr, pl.ds(0, cols)], prev_g[...], w1[0])
    gps[pl.ds(0, cols)] = gp
    for at in starts:
        here = pl.ds(at, step)
        if at + step < cells:
            xv = xd[jr, pl.ds(at + cols, step)]
        elif step > cols:
            xv = jnp.concatenate((xd[jr, pl.ds(at + cols, step - cols)], next_x[...]), 0)
        else:
            xv = next_x[...]
        both, gp, ga = edges(xd[jr, here], xv, gb[jr, here], w1[0])
        gps[pl.ds(at + cols, step)] = gp
        acc[here] += mm(jnp.concatenate((gp, gps[here]), 1), pw[jr])
        wacc[0] += weight_sums(gp, ga, both)

    feat = wacc.shape[2] // 4
    hidden = wacc.shape[1] // 2

    def reduce_out(kind):
        half = owners // 2
        g = wacc[kind]
        sd = jnp.concatenate((g[:hidden, :feat], g[:hidden, 2 * feat : 3 * feat]), 1)
        o = g[hidden:, 3 * feat :] - g[hidden:, feat : 2 * feat]
        o = jnp.concatenate((o[: hidden // 2], o[hidden // 2 :]), 1)
        part = jnp.concatenate((sd, o), 0).astype(BF16)
        wpart[pl.ds(kind * half, half)] = part.reshape(half, TILE, part.shape[1])

        for i in range(half):
            target = kind * half + lax.rem(flat + i, half)

            @pl.when(target != flat)
            def _(target=target):
                to = (lax.div(target, strips), lax.rem(target, strips))
                slot = lax.rem(flat - target + devices, devices) - 1
                send(wpart.at[target], wrecv.at[slot], red_send.at[0], red_recv.at[0], to)

    reduce_out(0)

    def arrived(ref, at):
        wide = ref[:, pl.ds(0, square), :].astype(F32).reshape(strips, rows, rows, ref.shape[2])
        first = at // cols
        parts = [wide[:, r].reshape(cols, ref.shape[2]) for r in range(first, first + chunk)]
        return jnp.concatenate(parts, 0).astype(BF16)

    @pl.when(p < pairs - 1)
    def _():
        wait_bytes(above, cross_recv.at[1])
        for at in starts:
            here = pl.ds(at, step)
            both, gp, ga = edges(xd[1, here], arrived(above, at), gb[3, here], w1[1])
            acc[here] += mm(gp, vw[1])
            wacc[1] += weight_sums(gp, ga, both)

    @pl.when(p > 0)
    def _():
        wait_bytes(below, cross_recv.at[0])
        lanes = below.shape[2]
        tile = below[:, pl.ds(square, TILE), :].astype(F32)
        pick = (
            lax.broadcasted_iota(jnp.int32, (rows, lanes), 0)
            == lax.broadcasted_iota(jnp.int32, (rows, lanes), 1)
        ).astype(F32)
        ones = jnp.ones((lanes, lanes), BF16)
        for at in starts:
            here = pl.ds(at, step)
            first = at // cols
            parts = [
                (tile[:, r : r + 1, :] * pick[None]).reshape(cols, lanes)
                for r in range(first, first + chunk)
            ]
            gate = mm(jnp.concatenate(parts, 0).astype(BF16), ones)
            _, gp, _ = edges(arrived(below, at), xd[0, here], gate, w1[1])
            acc[here] += mm(gp, vw[2])

    reduce_out(1)

    out_copy = pltpu.make_async_copy(acc, acc_out, in_sems.at[0])
    out_copy.start()

    @pl.when(flat < owners)
    def _():
        wait_bytes(wrecv, red_recv.at[0])
        total = jnp.sum(wrecv[...].astype(F32), 0) + wpart[flat].astype(F32)
        wres[flat] = total.astype(BF16)

        @pl.loop(1, devices)
        def _(k):
            send(wres.at[flat], wres.at[flat], red_send.at[1], red_recv.at[1], place(k)[1])

        few = pl.ds(0, owners - 1)
        wait_bytes(wres.at[few], red_recv.at[1])
        wait_bytes(wpart.at[few], red_send.at[0])
        wait_bytes(wrecv, red_send.at[1])

    @pl.when(flat >= owners)
    def _():
        wait_bytes(wres, red_recv.at[1])
        wait_bytes(wpart, red_send.at[0])

    @pl.when(p < pairs - 1)
    def _():
        wait_bytes(s_up, cross_send.at[0])

    @pl.when(p > 0)
    def _():
        wait_bytes(s_dn, cross_send.at[1])

    w_sum[...] = wres[...].astype(F32)
    out_copy.wait()


LANES = 128


def fetch(pairs_of_refs, sems, meanwhile=None):
    copies = [pltpu.make_async_copy(a, b, sems.at[i]) for i, (a, b) in enumerate(pairs_of_refs)]
    for copy in copies:
        copy.start()
    if meanwhile is not None:
        meanwhile()
    for copy in copies:
        copy.wait()


def stage_cells(
    pairs, strips, greet, ready, cross,
    nodes, up, usage, blockage, capacity, w_src, w_dst, w_out,
    xd, s_up, s_dn,
    nv, uv, usv, bv, cv, wsv, wdv, wov, t, q, sems,
):
    p = lax.axis_index("lyr")
    fetch(
        (
            (nodes, nv), (up, uv), (usage, usv), (blockage, bv), (capacity, cv),
            (w_src, wsv), (w_dst, wdv), (w_out, wov),
        ),
        sems,
        greet,
    )
    _, layers, feat, rows, cols = nv.shape
    lanes = 2 * feat
    half = feat * rows
    blocks = cols // LANES
    gates = (1 - bv[0, 1, 1]).astype(F32) * cv[0, 1, 1].astype(F32) * 0.25

    def spread(j, out):
        for r in range(rows):
            q[pl.ds(r, cols, stride=rows), :] = xd[j, pl.ds(r * cols, cols)].astype(F32)
        out[:, pl.ds(0, rows * rows), :] = q[...].astype(BF16).reshape(strips, rows * rows, lanes)

    leading = 1 - lax.rem(p, 2)
    for turn in range(layers):
        j = leading if turn == 0 else 1 - leading
        damp = lax.rsqrt(1.0 + usv[0, j].astype(F32))
        x = (nv[0, j].astype(F32) * damp[None]).astype(BF16).astype(F32)
        d = uv[0, j].astype(F32)
        for b in range(blocks):
            cut = slice(b * LANES, (b + 1) * LANES)
            t[b, pl.ds(0, half)] = x[:, :, cut].reshape(half, LANES)
            t[b, pl.ds(half, half)] = d[:, :, cut].reshape(half, LANES)
        for r in range(rows):
            for b in range(blocks):
                m = t[b, pl.ds(r, lanes, stride=rows), :]
                xd[j, pl.ds(r * cols + b * LANES, LANES)] = m.T.astype(BF16)

        @pl.when((j == 0) & (p > 0))
        def _():
            spread(0, s_dn)

        @pl.when((j == 1) & (p < pairs - 1))
        def _():
            spread(1, s_up)
            per = LANES // rows
            for b in range(blocks):
                g = gates[:, b * LANES : (b + 1) * LANES]
                g = jnp.concatenate((g, jnp.zeros((LANES - rows, LANES), F32)), 0).T
                g = g.reshape(per, rows, LANES)
                g = jnp.concatenate((g, jnp.zeros((per, TILE - rows, LANES), F32)), 1)
                s_up[pl.ds(b * per, per), pl.ds(rows * rows, TILE), :] = g.astype(BF16)

        if turn == 0:
            ready()
        cross(j)


def stage_rest(gb, w1, pw, vw, bv, cv, wsv, wdv, wov):
    p = lax.axis_index("lyr")
    s = lax.axis_index("strip")
    rows, cols = bv.shape[3:]
    feat = wsv.shape[1]
    lanes = 2 * feat
    blocks = cols // LANES
    gates = (1 - bv[0]).astype(F32) * cv[0].astype(F32) * 0.25
    row_ids = s * rows + lax.broadcasted_iota(jnp.int32, (rows, cols), 0)
    in_rows = (row_ids < cols - 1).astype(F32)
    in_cols = (lax.broadcasted_iota(jnp.int32, (rows, cols), 1) < cols - 1).astype(F32)
    odd = lax.rem(p, 2).astype(F32)
    low = (1.0 - odd) * in_rows + odd * in_cols
    high = odd * in_rows + (1.0 - odd) * in_cols
    four = (gates[0, 0] * low, gates[1, 0] * high, gates[0, 1], gates[1, 1])
    eye = (
        lax.broadcasted_iota(jnp.int32, (LANES, LANES), 0)
        == lax.broadcasted_iota(jnp.int32, (LANES, LANES), 1)
    ).astype(F32)
    ones = jnp.ones((LANES, lanes), BF16)
    for k, g in enumerate(four):
        parts = [
            (eye * g[r : r + 1, b * LANES : (b + 1) * LANES]).astype(BF16)
            for r in range(rows)
            for b in range(blocks)
        ]
        gb[k] = mm(jnp.concatenate(parts, 0), ones).astype(BF16)

    hidden = wsv.shape[2]
    zero = jnp.zeros((feat, hidden), BF16)
    for k in range(2):
        wo = wov[k]
        less = (-wo.astype(F32)).astype(BF16)
        w1[k, pl.ds(0, feat)] = jnp.concatenate((wsv[k], zero), 1)
        w1[k, pl.ds(feat, feat)] = jnp.concatenate((zero, less), 1)
        w1[k, pl.ds(2 * feat, feat)] = jnp.concatenate((wdv[k], zero), 1)
        w1[k, pl.ds(3 * feat, feat)] = jnp.concatenate((zero, wo), 1)
    none = jnp.zeros((hidden, feat), BF16)
    src, dst = [[v[k].astype(F32).T.astype(BF16) for k in range(2)] for v in (wsv, wdv)]
    for i, w in enumerate((src, dst)):
        here = pl.ds(i * hidden, hidden)
        pw[0, here] = jnp.concatenate((w[0], none), 1)
        pw[1, here] = jnp.concatenate((none, w[0]), 1)
    vw[0] = jnp.concatenate((src[1], dst[1]), 1)
    vw[1] = jnp.concatenate((none, src[1]), 1)
    vw[2] = jnp.concatenate((dst[1], none), 1)


def finish(scale, acc_in, w_in, up, usage, gn, gs, gd, go, acc, w_sum, uv, usv, t, sems):
    fetch(((acc_in, acc), (w_in, w_sum), (up, uv), (usage, usv)), sems)
    _, layers, feat, rows, cols = uv.shape
    lanes = 2 * feat
    half = feat * rows
    blocks = cols // LANES
    for b in range(blocks):
        for r in range(rows):
            t[b, pl.ds(r, lanes, stride=rows), :] = acc[pl.ds(r * cols + b * LANES, LANES)].T
    damp = lax.rsqrt(1.0 + usv[0].astype(F32))
    for j in range(layers):
        for b in range(blocks):
            cut = pl.ds(b * LANES, LANES)
            ns = t[b, pl.ds(j * half, half)].reshape(feat, rows, LANES)
            scaled = damp[j][None, :, b * LANES : (b + 1) * LANES] * ns
            gn[0, j, :, :, cut] = (uv[0, j, :, :, cut].astype(F32) + scaled).astype(BF16)
    hidden = gs.shape[2]
    w = w_sum[...].reshape(2, 3 * hidden // 2, lanes) * scale
    for k in range(2):
        sd = w[k, :hidden].T
        gs[k] = sd[:feat]
        gd[k] = sd[feat:]
        o = w[k, hidden:]
        go[k] = jnp.concatenate((o[:, :feat], o[:, feat:]), 0).T


def on_device(nodes, upstream, usage, blockage, capacity, w_src, w_dst, w_out):
    pairs = lax.axis_size("lyr")
    strips = lax.axis_size("strip")
    _, layers, feat, rows, cols = nodes.shape
    hidden = w_src.shape[1]
    cells = rows * cols
    lanes = 2 * feat
    owners = 2 * 3 * hidden * feat // (TILE * lanes)
    devices = pairs * strips
    chunk = max(1, min(rows, 1024 // cols))
    vmem = pl.BlockSpec(memory_space=pltpu.VMEM)
    hbm = pl.BlockSpec(memory_space=pltpu.HBM)
    params = pltpu.CompilerParams(vmem_limit_bytes=63 * 1024 * 1024)
    given = (nodes, upstream, usage, blockage, capacity)
    given += (jnp.swapaxes(w_src, 1, 2), jnp.swapaxes(w_dst, 1, 2), w_out)

    def shape(dims, kind=BF16):
        return jax.ShapeDtypeStruct(dims, kind)

    acc, w_sum = pl.pallas_call(
        functools.partial(kernel, pairs, strips, rows, cols, chunk),
        out_shape=(
            shape((cells, lanes), F32),
            jax.ShapeDtypeStruct((owners, TILE, lanes), F32),
        ),
        in_specs=[hbm] * 8,
        out_specs=(hbm, vmem),
        scratch_shapes=[
            pltpu.VMEM((cells, lanes), F32),
            pltpu.VMEM((layers, cells, lanes), BF16),
            pltpu.VMEM((strips, rows * rows + TILE, lanes), BF16),
            pltpu.VMEM((strips, rows * rows, lanes), BF16),
            pltpu.VMEM((4, cells, lanes), BF16),
            pltpu.VMEM((2, 4 * feat, 2 * hidden), BF16),
            pltpu.VMEM((2, 2 * hidden, lanes), BF16),
            pltpu.VMEM((3, hidden, lanes), BF16),
        ]
        + [pltpu.VMEM(a.shape, a.dtype) for a in given]
        + [
            pltpu.VMEM((cols // LANES, lanes * rows, LANES), F32),
            pltpu.VMEM((cells, lanes), F32),
            pltpu.SemaphoreType.DMA((8,)),
            pltpu.VMEM((cols, lanes), BF16),
            pltpu.VMEM((cols, lanes), BF16),
            pltpu.VMEM((cols, lanes), BF16),
            pltpu.VMEM((strips, rows * rows + TILE, lanes), BF16),
            pltpu.VMEM((strips, rows * rows, lanes), BF16),
            pltpu.VMEM((cells + cols, hidden), BF16),
            pltpu.VMEM((2, 2 * hidden, 4 * feat), F32),
            pltpu.VMEM((owners, TILE, lanes), BF16),
            pltpu.VMEM((devices - 1, TILE, lanes), BF16),
            pltpu.VMEM((owners, TILE, lanes), BF16),
            pltpu.SemaphoreType.DMA((3,)),
            pltpu.SemaphoreType.DMA((3,)),
            pltpu.SemaphoreType.DMA((2,)),
            pltpu.SemaphoreType.DMA((2,)),
            pltpu.SemaphoreType.DMA((2,)),
            pltpu.SemaphoreType.DMA((2,)),
        ],
        compiler_params=pltpu.CompilerParams(
            collective_id=0, has_side_effects=True, vmem_limit_bytes=63 * 1024 * 1024
        ),
    )(*given)

    scale = 1.0 / math.sqrt(2 * pairs * cols * cols)
    gn, gs, gd, go = pl.pallas_call(
        functools.partial(finish, scale),
        out_shape=(
            shape(nodes.shape),
            shape((2, feat, hidden), F32),
            shape((2, feat, hidden), F32),
            shape(w_out.shape, F32),
        ),
        in_specs=[hbm] * 4,
        out_specs=(vmem,) * 4,
        scratch_shapes=[
            pltpu.VMEM(acc.shape, acc.dtype),
            pltpu.VMEM(w_sum.shape, w_sum.dtype),
            pltpu.VMEM(upstream.shape, upstream.dtype),
            pltpu.VMEM(usage.shape, usage.dtype),
            pltpu.VMEM((cols // LANES, lanes * rows, LANES), F32),
            pltpu.SemaphoreType.DMA((4,)),
        ],
        compiler_params=params,
    )(acc, w_sum, upstream, usage)
    return gn, jnp.swapaxes(gs, 1, 2), jnp.swapaxes(gd, 1, 2), go


def solution(mesh):
    placed = (
        P("lyr", None, None, "strip", None),
        P("lyr", None, None, "strip", None),
        P("lyr", None, "strip", None),
        P("lyr", None, None, "strip", None),
        P("lyr", None, None, "strip", None),
        P(),
        P(),
        P(),
    )
    return jax.shard_map(
        on_device,
        mesh=mesh,
        in_specs=placed,
        out_specs=(P("lyr", None, None, "strip", None), P(), P(), P()),
        check_vma=False,
    )
```

```python
import functools
import math

import jax
import jax.numpy as jnp
from jax import lax
from jax.experimental import pallas as pl
from jax.experimental.pallas import tpu as pltpu
from jax.sharding import PartitionSpec as P

MESH = pl.DeviceIdType.MESH
F32 = jnp.float32
BF16 = jnp.bfloat16
TILE = 16


def mm(a, b):
    return jnp.dot(a, b, preferred_element_type=F32)


def edges(xu, xv, gate, w):
    both = jnp.concatenate((xu, xv), 1)
    y = mm(both, w)
    half = w.shape[1] // 2
    pre, raw = y[:, :half], y[:, half:]
    s = 0.5 * jnp.tanh(0.5 * pre) + 0.5
    act = pre * s
    slope = s + act * (1.0 - s)
    gate = gate.astype(F32)
    return both, (gate * raw * slope).astype(BF16), (gate * act).astype(BF16)


def weight_sums(gp, ga, both):
    left = jnp.concatenate((gp, ga), 1)
    return lax.dot_general(left, both, (((0,), (0,)), ((), ())), preferred_element_type=F32)


def kernel(
    pairs, strips, rows, cols, chunk,
    nodes, up, usage, blockage, capacity, w_src, w_dst, w_out,
    acc, w_sum,
    xd, s_up, s_dn, gb, w1, pw, vw,
    nv, uv, usv, bv, cv, wsv, wdv, wov, t_rows, q_rows, in_sems,
    prev_x, next_x, prev_g, below, above, gps, wacc, wpart, wrecv, wres,
    halo_send, halo_recv, cross_send, cross_recv, red_send, red_recv,
):
    p = lax.axis_index("lyr")
    s = lax.axis_index("strip")
    devices = pairs * strips
    flat = p * strips + s
    owners = wpart.shape[0]
    cells = rows * cols
    step = chunk * cols
    square = rows * rows

    def place(k):
        target = lax.rem(flat + k, devices)
        return target, (lax.div(target, strips), lax.rem(target, strips))

    barrier = pltpu.get_barrier_semaphore()

    def greet():
        @pl.loop(1, devices)
        def _(k):
            pl.semaphore_signal(barrier, inc=1, device_id=place(k)[1], device_id_type=MESH)

    stage(
        pairs, strips, greet,
        nodes, up, usage, blockage, capacity, w_src, w_dst, w_out,
        xd, s_up, s_dn, gb, w1, pw, vw,
        nv, uv, usv, bv, cv, wsv, wdv, wov, t_rows, q_rows, in_sems,
    )
    pl.semaphore_wait(barrier, devices - 1)

    jr = lax.rem(p, 2)
    jc = 1 - jr

    def send(src, dst, a, b, to):
        copy = pltpu.make_async_remote_copy(
            src_ref=src, dst_ref=dst, send_sem=a, recv_sem=b, device_id=to, device_id_type=MESH
        )
        copy.start()
        return copy

    def wait_bytes(ref, sem):
        pltpu.make_async_copy(ref, ref, sem).wait()

    after = (p, lax.rem(s + 1, strips))
    before = (p, lax.rem(s + strips - 1, strips))
    last = pl.ds(cells - cols, cols)
    halos = (
        send(xd.at[jr, pl.ds(0, cols)], next_x, halo_send.at[0], halo_recv.at[0], before),
        send(xd.at[jr, last], prev_x, halo_send.at[1], halo_recv.at[1], after),
        send(gb.at[jr, last], prev_g, halo_send.at[2], halo_recv.at[2], after),
    )

    @pl.loop(0, strips)
    def _(k):
        t = lax.rem(s + k, strips)

        @pl.when(p < pairs - 1)
        def _():
            send(s_up.at[t], below.at[s], cross_send.at[0], cross_recv.at[0], (p + 1, t))

        @pl.when(p > 0)
        def _():
            send(s_dn.at[t], above.at[s], cross_send.at[1], cross_recv.at[1], (p - 1, t))

    starts = range(0, cells, step)
    for at in starts:
        here = pl.ds(at, step)
        both, gp, ga = edges(xd[0, here], xd[1, here], gb[2, here], w1[1])
        acc[here] = mm(gp, vw[0])
        sums = weight_sums(gp, ga, both)
        wacc[1] = sums if at == 0 else wacc[1] + sums
    for at in starts:
        here = pl.ds(at, step)
        xu = xd[jc, here]
        wide = xu.astype(F32)
        xv = jnp.concatenate((wide[1:], wide[:1]), 0).astype(BF16)
        both, gp, ga = edges(xu, xv, gb[jc, here], w1[0])
        wide = gp.astype(F32)
        turned = jnp.concatenate((wide[-1:], wide[:-1]), 0).astype(BF16)
        acc[here] += mm(jnp.concatenate((gp, turned), 1), pw[jc])
        sums = weight_sums(gp, ga, both)
        wacc[0] = sums if at == 0 else wacc[0] + sums
    for copy in halos:
        copy.wait()
    _, gp, _ = edges(prev_x[...], xd[jr, pl.ds(0, cols)], prev_g[...], w1[0])
    gps[pl.ds(0, cols)] = gp
    for at in starts:
        here = pl.ds(at, step)
        if at + step < cells:
            xv = xd[jr, pl.ds(at + cols, step)]
        elif step > cols:
            xv = jnp.concatenate((xd[jr, pl.ds(at + cols, step - cols)], next_x[...]), 0)
        else:
            xv = next_x[...]
        both, gp, ga = edges(xd[jr, here], xv, gb[jr, here], w1[0])
        gps[pl.ds(at + cols, step)] = gp
        acc[here] += mm(jnp.concatenate((gp, gps[here]), 1), pw[jr])
        wacc[0] += weight_sums(gp, ga, both)

    feat = wacc.shape[2] // 4
    hidden = wacc.shape[1] // 2

    def reduce_out(kind):
        half = owners // 2
        g = wacc[kind]
        sd = jnp.concatenate((g[:hidden, :feat], g[:hidden, 2 * feat : 3 * feat]), 1)
        o = g[hidden:, 3 * feat :] - g[hidden:, feat : 2 * feat]
        o = jnp.concatenate((o[: hidden // 2], o[hidden // 2 :]), 1)
        part = jnp.concatenate((sd, o), 0).astype(BF16)
        wpart[pl.ds(kind * half, half)] = part.reshape(half, TILE, part.shape[1])

        @pl.loop(1, devices)
        def _(k):
            target, to = place(k)

            @pl.when((target >= kind * half) & (target < (kind + 1) * half))
            def _():
                send(wpart.at[target], wrecv.at[devices - 1 - k], red_send.at[0], red_recv.at[0], to)

    reduce_out(0)

    def arrived(ref, at):
        wide = ref[:, pl.ds(0, square), :].astype(F32).reshape(strips, rows, rows, ref.shape[2])
        first = at // cols
        parts = [wide[:, r].reshape(cols, ref.shape[2]) for r in range(first, first + chunk)]
        return jnp.concatenate(parts, 0).astype(BF16)

    @pl.when(p < pairs - 1)
    def _():
        wait_bytes(above, cross_recv.at[1])
        for at in starts:
            here = pl.ds(at, step)
            both, gp, ga = edges(xd[1, here], arrived(above, at), gb[3, here], w1[1])
            acc[here] += mm(gp, vw[1])
            wacc[1] += weight_sums(gp, ga, both)

    @pl.when(p > 0)
    def _():
        wait_bytes(below, cross_recv.at[0])
        lanes = below.shape[2]
        tile = below[:, pl.ds(square, TILE), :].astype(F32)
        pick = (
            lax.broadcasted_iota(jnp.int32, (rows, lanes), 0)
            == lax.broadcasted_iota(jnp.int32, (rows, lanes), 1)
        ).astype(F32)
        ones = jnp.ones((lanes, lanes), BF16)
        for at in starts:
            here = pl.ds(at, step)
            first = at // cols
            parts = [
                (tile[:, r : r + 1, :] * pick[None]).reshape(cols, lanes)
                for r in range(first, first + chunk)
            ]
            gate = mm(jnp.concatenate(parts, 0).astype(BF16), ones)
            _, gp, _ = edges(arrived(below, at), xd[0, here], gate, w1[1])
            acc[here] += mm(gp, vw[2])

    reduce_out(1)

    @pl.when(flat < owners)
    def _():
        wait_bytes(wrecv, red_recv.at[0])
        total = jnp.sum(wrecv[...].astype(F32), 0) + wpart[flat].astype(F32)
        wres[flat] = total.astype(BF16)

        @pl.loop(1, devices)
        def _(k):
            send(wres.at[flat], wres.at[flat], red_send.at[1], red_recv.at[1], place(k)[1])

        few = pl.ds(0, owners - 1)
        wait_bytes(wres.at[few], red_recv.at[1])
        wait_bytes(wpart.at[few], red_send.at[0])
        wait_bytes(wrecv, red_send.at[1])

    @pl.when(flat >= owners)
    def _():
        wait_bytes(wres, red_recv.at[1])
        wait_bytes(wpart, red_send.at[0])

    @pl.when(p < pairs - 1)
    def _():
        wait_bytes(s_up, cross_send.at[0])

    @pl.when(p > 0)
    def _():
        wait_bytes(s_dn, cross_send.at[1])

    w_sum[...] = wres[...].astype(F32)


LANES = 128


def fetch(pairs_of_refs, sems, meanwhile=None):
    copies = [pltpu.make_async_copy(a, b, sems.at[i]) for i, (a, b) in enumerate(pairs_of_refs)]
    for copy in copies:
        copy.start()
    if meanwhile is not None:
        meanwhile()
    for copy in copies:
        copy.wait()


def stage(
    pairs, strips, greet,
    nodes, up, usage, blockage, capacity, w_src, w_dst, w_out,
    xd, s_up, s_dn, gb, w1, pw, vw,
    nv, uv, usv, bv, cv, wsv, wdv, wov, t, q, sems,
):
    p = lax.axis_index("lyr")
    s = lax.axis_index("strip")
    fetch(
        (
            (nodes, nv), (up, uv), (usage, usv), (blockage, bv), (capacity, cv),
            (w_src, wsv), (w_dst, wdv), (w_out, wov),
        ),
        sems,
        greet,
    )
    _, layers, feat, rows, cols = nv.shape
    lanes = 2 * feat
    half = feat * rows
    blocks = cols // LANES
    damp = lax.rsqrt(1.0 + usv[0].astype(F32))
    for j in range(layers):
        x = (nv[0, j].astype(F32) * damp[j][None]).astype(BF16).astype(F32)
        d = uv[0, j].astype(F32)
        for b in range(blocks):
            cut = slice(b * LANES, (b + 1) * LANES)
            t[b, pl.ds(0, half)] = x[:, :, cut].reshape(half, LANES)
            t[b, pl.ds(half, half)] = d[:, :, cut].reshape(half, LANES)
        for r in range(rows):
            for b in range(blocks):
                m = t[b, pl.ds(r, lanes, stride=rows), :]
                xd[j, pl.ds(r * cols + b * LANES, LANES)] = m.T.astype(BF16)

    def spread(j, out):
        for r in range(rows):
            q[pl.ds(r, cols, stride=rows), :] = xd[j, pl.ds(r * cols, cols)].astype(F32)
        out[:, pl.ds(0, rows * rows), :] = q[...].astype(BF16).reshape(strips, rows * rows, lanes)

    @pl.when(p > 0)
    def _():
        spread(0, s_dn)

    gates = (1 - bv[0]).astype(F32) * cv[0].astype(F32) * 0.25

    @pl.when(p < pairs - 1)
    def _():
        spread(1, s_up)
        per = LANES // rows
        for b in range(blocks):
            g = gates[1, 1][:, b * LANES : (b + 1) * LANES]
            g = jnp.concatenate((g, jnp.zeros((LANES - rows, LANES), F32)), 0).T.reshape(per, rows, LANES)
            g = jnp.concatenate((g, jnp.zeros((per, TILE - rows, LANES), F32)), 1)
            s_up[pl.ds(b * per, per), pl.ds(rows * rows, TILE), :] = g.astype(BF16)

    row_ids = s * rows + lax.broadcasted_iota(jnp.int32, (rows, cols), 0)
    in_rows = (row_ids < cols - 1).astype(F32)
    in_cols = (lax.broadcasted_iota(jnp.int32, (rows, cols), 1) < cols - 1).astype(F32)
    odd = lax.rem(p, 2).astype(F32)
    low = (1.0 - odd) * in_rows + odd * in_cols
    high = odd * in_rows + (1.0 - odd) * in_cols
    four = (gates[0, 0] * low, gates[1, 0] * high, gates[0, 1], gates[1, 1])
    eye = (
        lax.broadcasted_iota(jnp.int32, (LANES, LANES), 0)
        == lax.broadcasted_iota(jnp.int32, (LANES, LANES), 1)
    ).astype(F32)
    ones = jnp.ones((LANES, lanes), BF16)
    for k, g in enumerate(four):
        parts = [
            (eye * g[r : r + 1, b * LANES : (b + 1) * LANES]).astype(BF16)
            for r in range(rows)
            for b in range(blocks)
        ]
        gb[k] = mm(jnp.concatenate(parts, 0), ones).astype(BF16)

    hidden = wsv.shape[2]
    zero = jnp.zeros((feat, hidden), BF16)
    for k in range(2):
        wo = wov[k]
        less = (-wo.astype(F32)).astype(BF16)
        w1[k, pl.ds(0, feat)] = jnp.concatenate((wsv[k], zero), 1)
        w1[k, pl.ds(feat, feat)] = jnp.concatenate((zero, less), 1)
        w1[k, pl.ds(2 * feat, feat)] = jnp.concatenate((wdv[k], zero), 1)
        w1[k, pl.ds(3 * feat, feat)] = jnp.concatenate((zero, wo), 1)
    none = jnp.zeros((hidden, feat), BF16)
    src, dst = [[v[k].astype(F32).T.astype(BF16) for k in range(2)] for v in (wsv, wdv)]
    for i, w in enumerate((src, dst)):
        here = pl.ds(i * hidden, hidden)
        pw[0, here] = jnp.concatenate((w[0], none), 1)
        pw[1, here] = jnp.concatenate((none, w[0]), 1)
    vw[0] = jnp.concatenate((src[1], dst[1]), 1)
    vw[1] = jnp.concatenate((none, src[1]), 1)
    vw[2] = jnp.concatenate((dst[1], none), 1)


def finish(scale, acc_in, w_in, up, usage, gn, gs, gd, go, acc, w_sum, uv, usv, t, sems):
    fetch(((acc_in, acc), (w_in, w_sum), (up, uv), (usage, usv)), sems)
    _, layers, feat, rows, cols = uv.shape
    lanes = 2 * feat
    half = feat * rows
    blocks = cols // LANES
    for b in range(blocks):
        for r in range(rows):
            t[b, pl.ds(r, lanes, stride=rows), :] = acc[pl.ds(r * cols + b * LANES, LANES)].T
    damp = lax.rsqrt(1.0 + usv[0].astype(F32))
    for j in range(layers):
        for b in range(blocks):
            cut = pl.ds(b * LANES, LANES)
            ns = t[b, pl.ds(j * half, half)].reshape(feat, rows, LANES)
            scaled = damp[j][None, :, b * LANES : (b + 1) * LANES] * ns
            gn[0, j, :, :, cut] = (uv[0, j, :, :, cut].astype(F32) + scaled).astype(BF16)
    hidden = gs.shape[2]
    w = w_sum[...].reshape(2, 3 * hidden // 2, lanes) * scale
    for k in range(2):
        sd = w[k, :hidden].T
        gs[k] = sd[:feat]
        gd[k] = sd[feat:]
        o = w[k, hidden:]
        go[k] = jnp.concatenate((o[:, :feat], o[:, feat:]), 0).T


def on_device(nodes, upstream, usage, blockage, capacity, w_src, w_dst, w_out):
    pairs = lax.axis_size("lyr")
    strips = lax.axis_size("strip")
    _, layers, feat, rows, cols = nodes.shape
    hidden = w_src.shape[1]
    cells = rows * cols
    lanes = 2 * feat
    owners = 2 * 3 * hidden * feat // (TILE * lanes)
    devices = pairs * strips
    chunk = max(1, min(rows, 1024 // cols))
    vmem = pl.BlockSpec(memory_space=pltpu.VMEM)
    hbm = pl.BlockSpec(memory_space=pltpu.HBM)
    params = pltpu.CompilerParams(vmem_limit_bytes=63 * 1024 * 1024)
    given = (nodes, upstream, usage, blockage, capacity)
    given += (jnp.swapaxes(w_src, 1, 2), jnp.swapaxes(w_dst, 1, 2), w_out)

    def shape(dims, kind=BF16):
        return jax.ShapeDtypeStruct(dims, kind)

    acc, w_sum = pl.pallas_call(
        functools.partial(kernel, pairs, strips, rows, cols, chunk),
        out_shape=(
            jax.ShapeDtypeStruct((cells, lanes), F32),
            jax.ShapeDtypeStruct((owners, TILE, lanes), F32),
        ),
        in_specs=[hbm] * 8,
        out_specs=(vmem, vmem),
        scratch_shapes=[
            pltpu.VMEM((layers, cells, lanes), BF16),
            pltpu.VMEM((strips, rows * rows + TILE, lanes), BF16),
            pltpu.VMEM((strips, rows * rows, lanes), BF16),
            pltpu.VMEM((4, cells, lanes), BF16),
            pltpu.VMEM((2, 4 * feat, 2 * hidden), BF16),
            pltpu.VMEM((2, 2 * hidden, lanes), BF16),
            pltpu.VMEM((3, hidden, lanes), BF16),
        ]
        + [pltpu.VMEM(a.shape, a.dtype) for a in given]
        + [
            pltpu.VMEM((cols // LANES, lanes * rows, LANES), F32),
            pltpu.VMEM((cells, lanes), F32),
            pltpu.SemaphoreType.DMA((8,)),
            pltpu.VMEM((cols, lanes), BF16),
            pltpu.VMEM((cols, lanes), BF16),
            pltpu.VMEM((cols, lanes), BF16),
            pltpu.VMEM((strips, rows * rows + TILE, lanes), BF16),
            pltpu.VMEM((strips, rows * rows, lanes), BF16),
            pltpu.VMEM((cells + cols, hidden), BF16),
            pltpu.VMEM((2, 2 * hidden, 4 * feat), F32),
            pltpu.VMEM((owners, TILE, lanes), BF16),
            pltpu.VMEM((devices - 1, TILE, lanes), BF16),
            pltpu.VMEM((owners, TILE, lanes), BF16),
            pltpu.SemaphoreType.DMA((3,)),
            pltpu.SemaphoreType.DMA((3,)),
            pltpu.SemaphoreType.DMA((2,)),
            pltpu.SemaphoreType.DMA((2,)),
            pltpu.SemaphoreType.DMA((2,)),
            pltpu.SemaphoreType.DMA((2,)),
        ],
        compiler_params=pltpu.CompilerParams(
            collective_id=0, has_side_effects=True, vmem_limit_bytes=63 * 1024 * 1024
        ),
    )(*given)

    scale = 1.0 / math.sqrt(2 * pairs * cols * cols)
    gn, gs, gd, go = pl.pallas_call(
        functools.partial(finish, scale),
        out_shape=(
            shape(nodes.shape),
            shape((2, feat, hidden), F32),
            shape((2, feat, hidden), F32),
            shape(w_out.shape, F32),
        ),
        in_specs=[hbm] * 4,
        out_specs=(vmem,) * 4,
        scratch_shapes=[
            pltpu.VMEM(acc.shape, acc.dtype),
            pltpu.VMEM(w_sum.shape, w_sum.dtype),
            pltpu.VMEM(upstream.shape, upstream.dtype),
            pltpu.VMEM(usage.shape, usage.dtype),
            pltpu.VMEM((cols // LANES, lanes * rows, LANES), F32),
            pltpu.SemaphoreType.DMA((4,)),
        ],
        compiler_params=params,
    )(acc, w_sum, upstream, usage)
    return gn, jnp.swapaxes(gs, 1, 2), jnp.swapaxes(gd, 1, 2), go


def solution(mesh):
    placed = (
        P("lyr", None, None, "strip", None),
        P("lyr", None, None, "strip", None),
        P("lyr", None, "strip", None),
        P("lyr", None, None, "strip", None),
        P("lyr", None, None, "strip", None),
        P(),
        P(),
        P(),
    )
    return jax.shard_map(
        on_device,
        mesh=mesh,
        in_specs=placed,
        out_specs=(P("lyr", None, None, "strip", None), P(), P(), P()),
        check_vma=False,
    )
```
